32 devices in a mesh: groups: 2 (over y), ctx: 4 (over z), seq: 2 (over x), head: 2 (over core).
Axes of the slice: x: 2, y: 2, z: 4, core: 2. Of those that a mesh axis runs over, the one named last changes fastest.
Arguments:
- queries: bfloat16 [4, 4, 128, 576], P(('groups', 'seq'), None, ('ctx', 'head')), parts along dimension 0, may hold values from -36 to 36
- cache: bfloat16 [4, 12288, 576], P(('groups', 'seq'), 'ctx'), parts along dimension 0, may hold values from -8 to 8
- lengths: int32 [4], P(('groups', 'seq')), parts along dimension 0, may hold values from 3072 to 12288, as said below
- offsets: int32 [4, 4], P(('groups', 'seq')), parts along dimension 0, may hold values from 0 to 3
- w_uv: bfloat16 [128, 512, 128], P(('ctx', 'head')), may hold values from -0.25 to 0.25
- w_out: bfloat16 [16384, 7168], P(('ctx', 'head'), 'seq'), may hold values from -0.046875 to 0.046875
Outputs:
- mixed: bfloat16 [16, 7168], P(('groups', 'ctx', 'head'), 'seq'), parts along dimension 0
The draws below stay inside these ranges and needn't reach their ends.
There are 2 independent parts, one for each index of `groups`. The reference program is written for one: setup_inputs(seed, part) draws one part's arguments, and reference() takes and returns one part's arrays. A program takes and returns all parts, laid end to end along the dimension named above; an argument that names none is the same for every part. Nothing has to cross between parts.
Inputs may be any that keep to these rules, and one draw needn't show every extreme that they name: `lengths`: each sequence's filled length, its 4 draft tokens included; some sequence reaches 12288 in every draw. Draft token t of sequence s sits at position lengths[s] - 4 + offsets[s, t].
All inputs are finite; a program needn't handle non-finite values.
Results may differ from the reference program's by a relative error of at most 0.014.
Values may be sent and summed in bfloat16 or wider, within the bound.
A program may use at most 64 MiB of HBM per device.

```python
import jax
import jax.numpy as jnp
from jax import lax

D = 7168
HEADS = 128
LATENT = 512
ROPE = 64
NOPE = 128
VDIM = 128
DRAFT = 4
SEQS = 2
LEN = 12288


def draw_cache(key, part):
    entries = LATENT + ROPE
    values = jnp.clip(jax.random.normal(jax.random.fold_in(key, 11), (SEQS, LEN, entries)), -4.5, 4.5)
    return values.astype(jnp.bfloat16)


def draw_queries(key, part):
    shape_all = (SEQS, DRAFT, HEADS, LATENT + ROPE)
    values = 2.0 * jnp.clip(jax.random.normal(jax.random.fold_in(key, 12), shape_all), -4.0, 4.0)
    return values.astype(jnp.bfloat16)


def draw_lengths(key, part):
    own_key = jax.random.fold_in(key, part)
    values = jax.random.randint(jax.random.fold_in(own_key, 21), (SEQS,), LEN // 4, LEN + 1)
    longest = jax.random.randint(jax.random.fold_in(own_key, 22), (), 0, SEQS)
    return jnp.where(jnp.arange(SEQS, dtype=jnp.int32) == longest, LEN, values).astype(jnp.int32)


def touch_ends(values, stream_key, low, top_value):
    place = [jax.random.randint(jax.random.fold_in(stream_key, axis), (), 0, length) for axis, length in enumerate(values.shape)]
    widest = values.shape.index(max(values.shape))
    neighbour = place[:widest] + [(place[widest] + 1) % values.shape[widest]] + place[widest + 1:]
    return values.at[tuple(place)].set(low).at[tuple(neighbour)].set(top_value)


def level_of(rng, dims, shards, smallest, largest):
    level = 1.0
    for dim, blocks in shards:
        heights = jax.random.uniform(jax.random.fold_in(jax.random.fold_in(rng, 6), dim), (blocks,), jnp.float32, smallest / len(shards), largest / len(shards))
        level = level * jnp.repeat(jnp.exp(heights), dims[dim] // blocks).reshape((-1,) + (1,) * (len(dims) - 1 - dim))
    return level


def noise(key, dims, width, bound, split=(), held_as=jnp.bfloat16):
    factor_of = level_of(key, dims, split, -0.22, 0.18) if split else 1.0
    drawn = jax.random.normal(key, dims, jnp.float32) * width * factor_of
    return jnp.minimum(jnp.maximum(drawn, -bound), bound).astype(held_as)


def setup_inputs(seed: int = 0, part: int = 0) -> dict:
    seeds = jax.random.split(jax.random.key(seed), 7)
    own_keys = jax.random.split(jax.random.fold_in(seeds[6], part), 7)
    return {
        "queries": draw_queries(jax.random.fold_in(jax.random.fold_in(seeds[6], part), 71), part),
        "cache": draw_cache(jax.random.fold_in(jax.random.fold_in(seeds[6], part), 71), part),
        "lengths": draw_lengths(jax.random.fold_in(jax.random.fold_in(seeds[6], part), 71), part),
        "offsets": touch_ends(jax.random.randint(own_keys[3], (SEQS, DRAFT), 0, DRAFT), jax.random.fold_in(own_keys[3], 1), 0, DRAFT - 1).astype(jnp.int32),
        "w_uv": noise(seeds[4], (HEADS, LATENT, VDIM), LATENT ** -0.5, 0.25, ((0, 8),)),
        "w_out": noise(seeds[5], (HEADS * VDIM, D), (HEADS * VDIM) ** -0.5, 0.046875, ((0, 8), (1, 2))),
    }


theta = 10000.0
negative = -1e30


def rotate(queries, positions):
    half_rope = ROPE // 2
    frequency = theta ** (-2.0 * jnp.arange(half_rope, dtype=jnp.float32) / ROPE)
    angles = positions.astype(jnp.float32)[..., None] * frequency
    cosine = jnp.cos(angles)[..., None, :]
    sine_part = jnp.sin(angles)[..., None, :]
    front_half = queries[..., LATENT:LATENT + half_rope].astype(jnp.float32)
    back_half = queries[..., LATENT + half_rope:].astype(jnp.float32)
    turned = jnp.concatenate([front_half * cosine - back_half * sine_part, back_half * cosine + front_half * sine_part], axis=-1)
    return jnp.concatenate([queries[..., :LATENT], turned.astype(jnp.bfloat16)], axis=-1)


def attend(packed):
    rotated, cache_rows, limits = packed
    flattened = rotated.reshape(DRAFT * HEADS, rotated.shape[-1])
    scores = lax.dot_general(flattened, cache_rows, (((1,), (1,)), ((), ())), preferred_element_type=jnp.float32) * (NOPE + ROPE) ** -0.5
    places = jnp.arange(cache_rows.shape[0], dtype=jnp.int32)
    bounds = jnp.repeat(limits, HEADS)
    visible = places[None, :] <= bounds[:, None]
    maxima = jnp.max(jnp.where(visible, scores, negative), axis=1, keepdims=True)
    weights = jnp.where(visible, jnp.exp(scores - maxima), 0.0)
    totals = jnp.sum(weights, axis=1, keepdims=True)
    numerators = jnp.dot(weights.astype(jnp.bfloat16), cache_rows[:, :LATENT], preferred_element_type=jnp.float32)
    return (numerators / totals).astype(jnp.bfloat16).reshape(DRAFT, HEADS, LATENT)


def reference(queries, cache, lengths, offsets, w_uv, w_out):
    positions = (lengths[:, None] - DRAFT + offsets).astype(jnp.int32)
    rotated = rotate(queries, positions)
    attended = lax.map(attend, (rotated, cache, positions))
    head_values = jnp.einsum("sthl,hlv->sthv", attended.astype(jnp.float32), w_uv.astype(jnp.float32)).astype(jnp.bfloat16)
    flattened = head_values.reshape(SEQS * DRAFT, HEADS * VDIM)
    return jnp.dot(flattened, w_out, preferred_element_type=jnp.float32).astype(jnp.bfloat16)
```

```python
import functools
import math

import jax
import jax.numpy as jnp
from jax import lax
from jax.experimental import pallas as pl
from jax.experimental.pallas import tpu as pltpu
from jax.sharding import PartitionSpec as P

ROPE = 64
NOPE = 128
DRAFT = 4
LANES = 128
THETA = 10000.0
NEGATIVE = -1e30
SCALE = (NOPE + ROPE) ** -0.5
TURN = 2.0 * math.pi
TURN_HIGH = 6.28125
TURN_MID = math.floor((TURN - TURN_HIGH) * 2**19) / 2**19
TURN_LOW = TURN - TURN_HIGH - TURN_MID
MESH = pl.DeviceIdType.MESH


def sine_cosine(angle):
    turns = jnp.floor(angle * (1.0 / TURN) + 0.5)
    r = ((angle - turns * TURN_HIGH) - turns * TURN_MID) - turns * TURN_LOW
    square = r * r
    sine = jnp.zeros_like(r)
    cosine = jnp.zeros_like(r)
    for i in range(9, -1, -1):
        sign = -1.0 if i % 2 else 1.0
        cosine = cosine * square + sign / math.factorial(2 * i)
        sine = sine * square + sign / math.factorial(2 * i + 1)
    return sine * r, cosine


def per_row(scalars, shape, per_token):
    row = lax.broadcasted_iota(jnp.int32, shape, 0)
    column = jnp.full(shape, scalars[-1])
    for t in range(len(scalars) - 2, -1, -1):
        column = jnp.where(row < (t + 1) * per_token, scalars[t], column)
    return column


def turned(rope, positions):
    rows = rope.shape[0]
    half = ROPE // 2
    lane = lax.broadcasted_iota(jnp.int32, (1, ROPE), 1)
    frequency = jnp.zeros((1, ROPE), jnp.float32)
    for i in range(half):
        frequency = jnp.where(lane % half == i, THETA ** (-2.0 * i / ROPE), frequency)
    position = per_row(positions, (rows, ROPE), rows // DRAFT).astype(jnp.float32)
    sine, cosine = sine_cosine(position * frequency)
    swapped = jnp.concatenate([rope[:, half:], rope[:, :half]], axis=1)
    return rope * cosine + jnp.where(lane < half, -swapped, swapped) * sine


def kernel(
    sizes,
    lengths, offsets, q_hbm, keys_hbm, w_uv_hbm, w_out_hbm,
    out,
    q_raw, q_all, keys, values, w_uv, w_out, own, part_out, part_in, lse_out, lse_in,
    attended, heads_all, sums, sums_out, sums_in,
    load_sem, q_send, q_recv, part_send, part_recv, lse_send, lse_recv,
    heads_send, heads_recv, sums_send, sums_recv,
):
    n_ctx, n_seq, n_head = sizes
    ctx, seq, head = lax.axis_index("ctx"), lax.axis_index("seq"), lax.axis_index("head")
    rows, entries = q_raw.shape
    latent, places = values.shape[1], values.shape[0]
    per_token = rows // DRAFT
    n_out = n_ctx * n_head
    place = ctx * n_head + head

    load_q = pltpu.make_async_copy(q_hbm, q_raw, load_sem.at[0])
    load_keys = pltpu.make_async_copy(keys_hbm, keys, load_sem.at[1])
    load_uv = pltpu.make_async_copy(w_uv_hbm, w_uv, load_sem.at[2])
    load_out = pltpu.make_async_copy(w_out_hbm, w_out, load_sem.at[3])
    load_q.start()
    load_keys.start()

    def row_device(k):
        other = lax.rem(place + k, n_out)
        return other, {"ctx": other // n_head, "head": lax.rem(other, n_head)}

    barrier = pltpu.get_barrier_semaphore()
    for k in range(1, n_out):
        pl.semaphore_signal(barrier, inc=1, device_id=row_device(k)[1], device_id_type=MESH)
    for k in range(1, n_seq):
        pl.semaphore_signal(
            barrier, inc=1, device_id={"seq": lax.rem(seq + k, n_seq)}, device_id_type=MESH
        )

    positions = [lengths[0] - DRAFT + offsets[0, t] for t in range(DRAFT)]
    limits = per_row(positions, (rows, 1), per_token)
    load_q.wait()
    latent_q = q_raw[:, :latent]
    rope_q = turned(q_raw[:, latent:].astype(jnp.float32), positions).astype(jnp.bfloat16)
    q_all[ctx, :, :latent] = latent_q
    q_all[ctx, :, latent:] = rope_q

    pl.semaphore_wait(barrier, n_out - 1 + n_seq - 1)

    step = jnp.where(ctx < n_ctx // 2, 1, n_ctx - 1)

    def peer(k):
        return lax.rem(ctx + k * step, n_ctx)

    def q_copy(k, slot):
        return pltpu.make_async_remote_copy(
            src_ref=q_all.at[ctx], dst_ref=q_all.at[slot],
            send_sem=q_send.at[k], recv_sem=q_recv.at[slot],
            device_id={"ctx": peer(k)}, device_id_type=MESH,
        )

    def part_copy(k, slot):
        return pltpu.make_async_remote_copy(
            src_ref=part_out.at[k], dst_ref=part_in.at[slot],
            send_sem=part_send.at[k], recv_sem=part_recv.at[slot],
            device_id={"ctx": peer(k)}, device_id_type=MESH,
        )

    def lse_copy(k, slot):
        return pltpu.make_async_remote_copy(
            src_ref=lse_out.at[k], dst_ref=lse_in.at[slot],
            send_sem=lse_send.at[k], recv_sem=lse_recv.at[slot],
            device_id={"ctx": peer(k)}, device_id_type=MESH,
        )

    for k in range(1, n_ctx):
        q_copy(k, ctx).start()

    load_keys.wait()
    load_uv.start()
    load_out.start()
    tile = 512
    for first in range(0, places, tile):
        values[first : first + tile, :] = keys[:latent, first : first + tile].T

    first_place = ctx * places

    def attend(block):
        scores = jnp.dot(block, keys[...], preferred_element_type=jnp.float32)
        place_of = first_place + lax.broadcasted_iota(jnp.int32, scores.shape, 1)
        scores = jnp.where(place_of <= limits, scores, NEGATIVE)
        maxima = jnp.max(scores, axis=1, keepdims=True)
        weights = jnp.exp((scores - maxima) * SCALE)
        totals = jnp.sum(weights, axis=1, keepdims=True)
        numerators = jnp.dot(
            weights.astype(jnp.bfloat16), values[...], preferred_element_type=jnp.float32
        )
        return numerators / totals, maxima * SCALE + jnp.log(totals)

    diagonal = lax.broadcasted_iota(jnp.int32, (rows, rows), 0) == lax.broadcasted_iota(
        jnp.int32, (rows, rows), 1
    )

    own_part, own_lse = attend(q_all[ctx])
    own[...] = own_part

    def remote_block(k, carried):
        owner = peer(k)
        q_copy(k, owner).wait_recv()
        part, lse = attend(q_all[owner])
        part_out[k] = part.astype(jnp.bfloat16)
        as_row = jnp.sum(jnp.where(diagonal, lse, 0.0), axis=0, keepdims=True)
        lse_out[k] = jnp.broadcast_to(as_row, lse_out.shape[1:])
        part_copy(k, ctx).start()
        lse_copy(k, ctx).start()
        return carried

    lax.fori_loop(1, n_ctx, remote_block, 0)

    top = own_lse
    lses = []
    for k in range(1, n_ctx):
        slot = peer(k)
        lse_copy(k, slot).wait_recv()
        lse = jnp.sum(
            jnp.where(diagonal, lse_in[slot, 0:1, :], 0.0), axis=1, keepdims=True
        )
        lses.append(lse)
        top = jnp.maximum(top, lse)
    share = jnp.exp(own_lse - top)
    whole = share
    mixed = own[...] * share
    for k in range(1, n_ctx):
        slot = peer(k)
        part_copy(k, slot).wait_recv()
        share = jnp.exp(lses[k - 1] - top)
        whole = whole + share
        mixed = mixed + part_in[slot].astype(jnp.float32) * share
    mixed = mixed / whole
    for t in range(DRAFT):
        attended[t] = mixed[t * per_token : (t + 1) * per_token]

    load_uv.wait()
    vdim = w_uv.shape[2]
    for h in range(per_token):
        heads_all[seq, :, h * vdim : (h + 1) * vdim] = jnp.dot(
            attended[:, h, :].astype(jnp.bfloat16), w_uv[h], preferred_element_type=jnp.float32
        )

    def heads_copy(k, slot):
        return pltpu.make_async_remote_copy(
            src_ref=heads_all.at[seq], dst_ref=heads_all.at[slot],
            send_sem=heads_send.at[k], recv_sem=heads_recv.at[slot],
            device_id={"seq": lax.rem(seq + k, n_seq)}, device_id_type=MESH,
        )

    for k in range(1, n_seq):
        heads_copy(k, seq).start()
    columns = w_out.shape[1]
    n_blocks = columns // LANES
    sums[...] = jnp.zeros_like(sums)
    load_out.wait()
    for k in range(1, n_seq):
        heads_copy(k, lax.rem(seq + k, n_seq)).wait_recv()
    tokens = jnp.concatenate([heads_all[s] for s in range(n_seq)], axis=0).astype(jnp.bfloat16)
    width = 512 if columns % 512 == 0 else LANES
    for first in range(0, columns, width):
        product = jnp.dot(
            tokens, w_out[:, first : first + width], preferred_element_type=jnp.float32
        )
        for r in range(n_out):
            for i in range(width // LANES):
                sums[r, first // LANES + i, :] = product[r, i * LANES : (i + 1) * LANES]

    def sums_copy(k, target, slot):
        return pltpu.make_async_remote_copy(
            src_ref=sums_out.at[target], dst_ref=sums_in.at[slot],
            send_sem=sums_send.at[k], recv_sem=sums_recv.at[slot],
            device_id=row_device(k)[1], device_id_type=MESH,
        )

    for k in range(1, n_out):
        target = row_device(k)[0]
        sums_out[target] = sums[target].astype(jnp.bfloat16)
        sums_copy(k, target, place).start()
    result = sums[place]
    for k in range(1, n_out):
        slot = row_device(k)[0]
        sums_copy(k, slot, slot).wait_recv()
        result = result + sums_in[slot].astype(jnp.float32)
    out[...] = result[:n_blocks].astype(jnp.bfloat16)

    for k in range(1, n_ctx):
        q_copy(k, ctx).wait_send()
        part_copy(k, ctx).wait_send()
        lse_copy(k, ctx).wait_send()
    for k in range(1, n_seq):
        heads_copy(k, seq).wait_send()
    for k in range(1, n_out):
        sums_copy(k, row_device(k)[0], place).wait_send()


def per_device(sizes, queries, cache, lengths, offsets, w_uv, w_out):
    n_ctx, n_seq, n_head = sizes
    n_out = n_ctx * n_head
    heads, entries = queries.shape[2:]
    rows = DRAFT * heads
    places = cache.shape[1]
    latent, vdim = w_uv.shape[1:]
    columns = w_out.shape[1]
    n_blocks = columns // LANES
    padded = -(-n_blocks // 16) * 16
    sixteen, full = jnp.bfloat16, jnp.float32
    dma = pltpu.SemaphoreType.DMA
    smem = pl.BlockSpec(memory_space=pltpu.SMEM)
    anywhere = pl.BlockSpec(memory_space=pl.ANY)
    mixed = pl.pallas_call(
        functools.partial(kernel, sizes),
        out_shape=jax.ShapeDtypeStruct((n_blocks, LANES), sixteen),
        in_specs=[smem, smem, anywhere, anywhere, anywhere, anywhere],
        out_specs=pl.BlockSpec(memory_space=pltpu.VMEM),
        scratch_shapes=[
            pltpu.VMEM((rows, entries), sixteen),
            pltpu.VMEM((n_ctx, rows, entries), sixteen),
            pltpu.VMEM((entries, places), sixteen),
            pltpu.VMEM((places, latent), sixteen),
            pltpu.VMEM(w_uv.shape, sixteen),
            pltpu.VMEM(w_out.shape, sixteen),
            pltpu.VMEM((rows, latent), full),
            pltpu.VMEM((n_ctx, rows, latent), sixteen),
            pltpu.VMEM((n_ctx, rows, latent), sixteen),
            pltpu.VMEM((n_ctx, 8, rows), full),
            pltpu.VMEM((n_ctx, 8, rows), full),
            pltpu.VMEM((DRAFT, heads, latent), full),
            pltpu.VMEM((n_seq, DRAFT, heads * vdim), full),
            pltpu.VMEM((n_out, padded, LANES), full),
            pltpu.VMEM((n_out, padded, LANES), sixteen),
            pltpu.VMEM((n_out, padded, LANES), sixteen),
            dma((4,)),
            dma((n_ctx,)), dma((n_ctx,)),
            dma((n_ctx,)), dma((n_ctx,)),
            dma((n_ctx,)), dma((n_ctx,)),
            dma((n_seq,)), dma((n_seq,)),
            dma((n_out,)), dma((n_out,)),
        ],
        compiler_params=pltpu.CompilerParams(
            collective_id=0, has_side_effects=True, vmem_limit_bytes=60 * 2**20
        ),
        name="latent_attention",
    )(
        lengths,
        offsets,
        queries.reshape(rows, entries),
        jnp.swapaxes(cache[0], 0, 1),
        w_uv,
        w_out,
    )
    return mixed.reshape(1, columns)


def solution(mesh):
    sizes = (mesh.shape["ctx"], mesh.shape["seq"], mesh.shape["head"])
    in_specs = (
        P(("groups", "seq"), None, ("ctx", "head"), None),
        P(("groups", "seq"), "ctx", None),
        P(("groups", "seq")),
        P(("groups", "seq"), None),
        P(("ctx", "head"), None, None),
        P(("ctx", "head"), "seq"),
    )
    out_specs = P(("groups", "ctx", "head"), "seq")
    return jax.shard_map(
        functools.partial(per_device, sizes),
        mesh=mesh, in_specs=in_specs, out_specs=out_specs, check_vma=False,
    )
```

```python
import functools
import math

import jax
import jax.numpy as jnp
from jax import lax
from jax.experimental import pallas as pl
from jax.experimental.pallas import tpu as pltpu
from jax.sharding import PartitionSpec as P

ROPE = 64
NOPE = 128
DRAFT = 4
LANES = 128
THETA = 10000.0
NEGATIVE = -1e30
SCALE = (NOPE + ROPE) ** -0.5
TURN = 2.0 * math.pi
TURN_HIGH = 6.28125
TURN_MID = math.floor((TURN - TURN_HIGH) * 2**19) / 2**19
TURN_LOW = TURN - TURN_HIGH - TURN_MID
MESH = pl.DeviceIdType.MESH


def sine_cosine(angle):
    turns = jnp.floor(angle * (1.0 / TURN) + 0.5)
    r = ((angle - turns * TURN_HIGH) - turns * TURN_MID) - turns * TURN_LOW
    square = r * r
    sine = jnp.zeros_like(r)
    cosine = jnp.zeros_like(r)
    for i in range(9, -1, -1):
        sign = -1.0 if i % 2 else 1.0
        cosine = cosine * square + sign / math.factorial(2 * i)
        sine = sine * square + sign / math.factorial(2 * i + 1)
    return sine * r, cosine


def per_row(scalars, shape, per_token):
    row = lax.broadcasted_iota(jnp.int32, shape, 0)
    column = jnp.full(shape, scalars[-1])
    for t in range(len(scalars) - 2, -1, -1):
        column = jnp.where(row < (t + 1) * per_token, scalars[t], column)
    return column


def turned(rope, positions):
    rows = rope.shape[0]
    half = ROPE // 2
    lane = lax.broadcasted_iota(jnp.int32, (1, ROPE), 1)
    frequency = jnp.zeros((1, ROPE), jnp.float32)
    for i in range(half):
        frequency = jnp.where(lane % half == i, THETA ** (-2.0 * i / ROPE), frequency)
    position = per_row(positions, (rows, ROPE), rows // DRAFT).astype(jnp.float32)
    sine, cosine = sine_cosine(position * frequency)
    swapped = jnp.concatenate([rope[:, half:], rope[:, :half]], axis=1)
    return rope * cosine + jnp.where(lane < half, -swapped, swapped) * sine


def kernel(
    sizes,
    lengths, offsets, q_hbm, keys_hbm, w_uv_hbm, w_out_hbm,
    out,
    q_raw, q_all, keys, w_uv, w_out, own, part_out, part_in, lse_out, lse_in,
    attended, heads_all, sums, sums_out, sums_in,
    load_sem, q_send, q_recv, part_send, part_recv, lse_send, lse_recv,
    heads_send, heads_recv, sums_send, sums_recv,
):
    n_ctx, n_seq, n_head = sizes
    ctx, seq, head = lax.axis_index("ctx"), lax.axis_index("seq"), lax.axis_index("head")
    rows, entries = q_raw.shape
    latent, places = own.shape[1], keys.shape[1]
    per_token = rows // DRAFT
    n_out = n_ctx * n_head
    place = ctx * n_head + head

    load_q = pltpu.make_async_copy(q_hbm, q_raw, load_sem.at[0])
    load_keys = pltpu.make_async_copy(keys_hbm, keys, load_sem.at[1])
    load_uv = pltpu.make_async_copy(w_uv_hbm, w_uv, load_sem.at[2])
    load_out = pltpu.make_async_copy(w_out_hbm, w_out, load_sem.at[3])
    load_q.start()
    load_keys.start()

    def row_device(k):
        other = lax.rem(place + k, n_out)
        return other, {"ctx": other // n_head, "head": lax.rem(other, n_head)}

    barrier = pltpu.get_barrier_semaphore()
    for k in range(1, n_out):
        pl.semaphore_signal(barrier, inc=1, device_id=row_device(k)[1], device_id_type=MESH)
    for k in range(1, n_seq):
        pl.semaphore_signal(
            barrier, inc=1, device_id={"seq": lax.rem(seq + k, n_seq)}, device_id_type=MESH
        )

    positions = [lengths[0] - DRAFT + offsets[0, t] for t in range(DRAFT)]
    limits = per_row(positions, (rows, 1), per_token)
    load_q.wait()
    latent_q = q_raw[:, :latent]
    rope_q = turned(q_raw[:, latent:].astype(jnp.float32), positions).astype(jnp.bfloat16)
    q_all[ctx, :, :latent] = latent_q
    q_all[ctx, :, latent:] = rope_q

    pl.semaphore_wait(barrier, n_out - 1 + n_seq - 1)

    step = jnp.where(ctx < n_ctx // 2, 1, n_ctx - 1)

    def peer(k):
        return lax.rem(ctx + k * step, n_ctx)

    def q_copy(k, slot):
        return pltpu.make_async_remote_copy(
            src_ref=q_all.at[ctx], dst_ref=q_all.at[slot],
            send_sem=q_send.at[k], recv_sem=q_recv.at[slot],
            device_id={"ctx": peer(k)}, device_id_type=MESH,
        )

    def part_copy(k, slot):
        return pltpu.make_async_remote_copy(
            src_ref=part_out.at[k], dst_ref=part_in.at[slot],
            send_sem=part_send.at[k], recv_sem=part_recv.at[slot],
            device_id={"ctx": peer(k)}, device_id_type=MESH,
        )

    def lse_copy(k, slot):
        return pltpu.make_async_remote_copy(
            src_ref=lse_out.at[k], dst_ref=lse_in.at[slot],
            send_sem=lse_send.at[k], recv_sem=lse_recv.at[slot],
            device_id={"ctx": peer(k)}, device_id_type=MESH,
        )

    for k in range(1, n_ctx):
        q_copy(k, ctx).start()

    load_keys.wait()
    load_uv.start()
    load_out.start()
    first_place = ctx * places

    def attend(block):
        scores = jnp.dot(block, keys[...], preferred_element_type=jnp.float32)
        place_of = first_place + lax.broadcasted_iota(jnp.int32, scores.shape, 1)
        scores = jnp.where(place_of <= limits, scores, NEGATIVE)
        maxima = jnp.max(scores, axis=1, keepdims=True)
        weights = jnp.exp((scores - maxima) * SCALE)
        totals = jnp.sum(weights, axis=1, keepdims=True)
        numerators = lax.dot_general(
            weights.astype(jnp.bfloat16), keys[:latent, :], (((1,), (1,)), ((), ())),
            preferred_element_type=jnp.float32,
        )
        return numerators / totals, maxima * SCALE + jnp.log(totals)

    diagonal = lax.broadcasted_iota(jnp.int32, (rows, rows), 0) == lax.broadcasted_iota(
        jnp.int32, (rows, rows), 1
    )

    own_part, own_lse = attend(q_all[ctx])
    own[...] = own_part

    def remote_block(k, carried):
        owner = peer(k)
        q_copy(k, owner).wait_recv()
        part, lse = attend(q_all[owner])
        part_out[k] = part.astype(jnp.bfloat16)
        as_row = jnp.sum(jnp.where(diagonal, lse, 0.0), axis=0, keepdims=True)
        lse_out[k] = jnp.broadcast_to(as_row, lse_out.shape[1:])
        part_copy(k, ctx).start()
        lse_copy(k, ctx).start()
        return carried

    lax.fori_loop(1, n_ctx, remote_block, 0)

    top = own_lse
    lses = []
    for k in range(1, n_ctx):
        slot = peer(k)
        lse_copy(k, slot).wait_recv()
        lse = jnp.sum(
            jnp.where(diagonal, lse_in[slot, 0:1, :], 0.0), axis=1, keepdims=True
        )
        lses.append(lse)
        top = jnp.maximum(top, lse)
    share = jnp.exp(own_lse - top)
    whole = share
    mixed = own[...] * share
    for k in range(1, n_ctx):
        slot = peer(k)
        part_copy(k, slot).wait_recv()
        share = jnp.exp(lses[k - 1] - top)
        whole = whole + share
        mixed = mixed + part_in[slot].astype(jnp.float32) * share
    mixed = mixed / whole
    for t in range(DRAFT):
        attended[t] = mixed[t * per_token : (t + 1) * per_token]

    load_uv.wait()
    vdim = w_uv.shape[2]
    for h in range(per_token):
        heads_all[seq, :, h * vdim : (h + 1) * vdim] = jnp.dot(
            attended[:, h, :].astype(jnp.bfloat16), w_uv[h], preferred_element_type=jnp.float32
        )

    def heads_copy(k, slot):
        return pltpu.make_async_remote_copy(
            src_ref=heads_all.at[seq], dst_ref=heads_all.at[slot],
            send_sem=heads_send.at[k], recv_sem=heads_recv.at[slot],
            device_id={"seq": lax.rem(seq + k, n_seq)}, device_id_type=MESH,
        )

    for k in range(1, n_seq):
        heads_copy(k, seq).start()
    columns = w_out.shape[1]
    n_parts = sums.shape[0]
    part_columns = columns // n_parts
    part_blocks = part_columns // LANES
    sums[...] = jnp.zeros_like(sums)
    load_out.wait()
    for k in range(1, n_seq):
        heads_copy(k, lax.rem(seq + k, n_seq)).wait_recv()
    tokens = jnp.concatenate([heads_all[s] for s in range(n_seq)], axis=0).astype(jnp.bfloat16)
    width = 2 * LANES if part_columns % (2 * LANES) == 0 else LANES

    def sums_copy(part, k, target, slot):
        return pltpu.make_async_remote_copy(
            src_ref=sums_out.at[part, target], dst_ref=sums_in.at[part, slot],
            send_sem=sums_send.at[part, k], recv_sem=sums_recv.at[part, slot],
            device_id=row_device(k)[1], device_id_type=MESH,
        )

    for part in range(n_parts):
        for first in range(0, part_columns, width):
            begin = part * part_columns + first
            product = jnp.dot(
                tokens, w_out[:, begin : begin + width], preferred_element_type=jnp.float32
            )
            for r in range(n_out):
                for i in range(width // LANES):
                    sums[part, r, first // LANES + i, :] = product[r, i * LANES : (i + 1) * LANES]
        for k in range(1, n_out):
            target = row_device(k)[0]
            sums_out[part, target] = sums[part, target].astype(jnp.bfloat16)
            sums_copy(part, k, target, place).start()
    for part in range(n_parts):
        result = sums[part, place]
        for k in range(1, n_out):
            slot = row_device(k)[0]
            sums_copy(part, k, slot, slot).wait_recv()
            result = result + sums_in[part, slot].astype(jnp.float32)
        for i in range(part_blocks):
            begin = part * part_columns + i * LANES
            out[:, begin : begin + LANES] = result[i : i + 1].astype(jnp.bfloat16)

    for k in range(1, n_ctx):
        q_copy(k, ctx).wait_send()
        part_copy(k, ctx).wait_send()
        lse_copy(k, ctx).wait_send()
    for k in range(1, n_seq):
        heads_copy(k, seq).wait_send()
    for part in range(n_parts):
        for k in range(1, n_out):
            sums_copy(part, k, row_device(k)[0], place).wait_send()


def per_device(sizes, queries, cache, lengths, offsets, w_uv, w_out):
    n_ctx, n_seq, n_head = sizes
    n_out = n_ctx * n_head
    heads, entries = queries.shape[2:]
    rows = DRAFT * heads
    places = cache.shape[1]
    latent, vdim = w_uv.shape[1:]
    columns = w_out.shape[1]
    n_blocks = columns // LANES
    n_parts = 2 if n_blocks % 2 == 0 else 1
    padded = -(-n_blocks // n_parts // 16) * 16
    sixteen, full = jnp.bfloat16, jnp.float32
    dma = pltpu.SemaphoreType.DMA
    smem = pl.BlockSpec(memory_space=pltpu.SMEM)
    anywhere = pl.BlockSpec(memory_space=pl.ANY)
    return pl.pallas_call(
        functools.partial(kernel, sizes),
        out_shape=jax.ShapeDtypeStruct((1, columns), sixteen),
        in_specs=[smem, smem, anywhere, anywhere, anywhere, anywhere],
        out_specs=pl.BlockSpec(memory_space=pltpu.VMEM),
        scratch_shapes=[
            pltpu.VMEM((rows, entries), sixteen),
            pltpu.VMEM((n_ctx, rows, entries), sixteen),
            pltpu.VMEM((entries, places), sixteen),
            pltpu.VMEM(w_uv.shape, sixteen),
            pltpu.VMEM(w_out.shape, sixteen),
            pltpu.VMEM((rows, latent), full),
            pltpu.VMEM((n_ctx, rows, latent), sixteen),
            pltpu.VMEM((n_ctx, rows, latent), sixteen),
            pltpu.VMEM((n_ctx, 8, rows), full),
            pltpu.VMEM((n_ctx, 8, rows), full),
            pltpu.VMEM((DRAFT, heads, latent), full),
            pltpu.VMEM((n_seq, DRAFT, heads * vdim), full),
            pltpu.VMEM((n_parts, n_out, padded, LANES), full),
            pltpu.VMEM((n_parts, n_out, padded, LANES), sixteen),
            pltpu.VMEM((n_parts, n_out, padded, LANES), sixteen),
            dma((4,)),
            dma((n_ctx,)), dma((n_ctx,)),
            dma((n_ctx,)), dma((n_ctx,)),
            dma((n_ctx,)), dma((n_ctx,)),
            dma((n_seq,)), dma((n_seq,)),
            dma((n_parts, n_out)), dma((n_parts, n_out)),
        ],
        compiler_params=pltpu.CompilerParams(
            collective_id=0, has_side_effects=True, vmem_limit_bytes=60 * 2**20
        ),
        name="latent_attention",
    )(
        lengths,
        offsets,
        queries.reshape(rows, entries),
        jnp.swapaxes(cache[0], 0, 1),
        w_uv,
        w_out,
    )


def solution(mesh):
    sizes = (mesh.shape["ctx"], mesh.shape["seq"], mesh.shape["head"])
    in_specs = (
        P(("groups", "seq"), None, ("ctx", "head"), None),
        P(("groups", "seq"), "ctx", None),
        P(("groups", "seq")),
        P(("groups", "seq"), None),
        P(("ctx", "head"), None, None),
        P(("ctx", "head"), "seq"),
    )
    out_specs = P(("groups", "ctx", "head"), "seq")
    return jax.shard_map(
        functools.partial(per_device, sizes),
        mesh=mesh, in_specs=in_specs, out_specs=out_specs, check_vma=False,
    )
```

```python
import functools
import math

import jax
import jax.numpy as jnp
from jax import lax
from jax.experimental import pallas as pl
from jax.experimental.pallas import tpu as pltpu
from jax.sharding import PartitionSpec as P

ROPE = 64
NOPE = 128
DRAFT = 4
LANES = 128
THETA = 10000.0
NEGATIVE = -1e30
SCALE = (NOPE + ROPE) ** -0.5
LN2 = math.log(2.0)
TURN = 2.0 * math.pi
TURN_HIGH = 6.28125
TURN_MID = math.floor((TURN - TURN_HIGH) * 2**19) / 2**19
TURN_LOW = TURN - TURN_HIGH - TURN_MID
MESH = pl.DeviceIdType.MESH


def sine_cosine(angle):
    turns = jnp.floor(angle * (1.0 / TURN) + 0.5)
    r = ((angle - turns * TURN_HIGH) - turns * TURN_MID) - turns * TURN_LOW
    square = r * r
    sine = jnp.zeros_like(r)
    cosine = jnp.zeros_like(r)
    for i in range(9, -1, -1):
        sign = -1.0 if i % 2 else 1.0
        cosine = cosine * square + sign / math.factorial(2 * i)
        sine = sine * square + sign / math.factorial(2 * i + 1)
    return sine * r, cosine


def per_row(scalars, shape, per_token):
    row = lax.broadcasted_iota(jnp.int32, shape, 0)
    column = jnp.full(shape, scalars[-1])
    for t in range(len(scalars) - 2, -1, -1):
        column = jnp.where(row < (t + 1) * per_token, scalars[t], column)
    return column


def turned(rope, positions):
    rows = rope.shape[0]
    half = ROPE // 2
    lane = lax.broadcasted_iota(jnp.int32, (1, ROPE), 1)
    frequency = jnp.zeros((1, ROPE), jnp.float32)
    for i in range(half):
        frequency = jnp.where(lane % half == i, THETA ** (-2.0 * i / ROPE), frequency)
    position = per_row(positions, (rows, ROPE), rows // DRAFT).astype(jnp.float32)
    sine, cosine = sine_cosine(position * frequency)
    swapped = jnp.concatenate([rope[:, half:], rope[:, :half]], axis=1)
    return rope * cosine + jnp.where(lane < half, -swapped, swapped) * sine


def kernel(
    sizes,
    lengths, offsets, q_hbm, keys_hbm, w_uv_hbm, w_out_hbm,
    out,
    q_raw, q_all, keys, w_uv, w_out, own, part_out, part_in, lse_out, lse_in,
    attended, heads_all, sums, sums_out, sums_in,
    load_sem, q_send, q_recv, part_send, part_recv, lse_send, lse_recv,
    heads_send, heads_recv, sums_send, sums_recv,
):
    n_ctx, n_seq, n_head = sizes
    ctx, seq, head = lax.axis_index("ctx"), lax.axis_index("seq"), lax.axis_index("head")
    rows, entries = q_raw.shape
    latent, places = own.shape[1], keys.shape[1]
    per_token = rows // DRAFT
    n_out = n_ctx * n_head
    place = ctx * n_head + head

    load_q = pltpu.make_async_copy(q_hbm, q_raw, load_sem.at[0])
    load_keys = pltpu.make_async_copy(keys_hbm, keys, load_sem.at[1])
    load_uv = pltpu.make_async_copy(w_uv_hbm, w_uv, load_sem.at[2])
    load_out = pltpu.make_async_copy(w_out_hbm, w_out, load_sem.at[3])
    load_q.start()
    load_keys.start()

    def row_device(k):
        other = lax.rem(place + k, n_out)
        return other, {"ctx": other // n_head, "head": lax.rem(other, n_head)}

    barrier = pltpu.get_barrier_semaphore()
    for k in range(1, n_out):
        pl.semaphore_signal(barrier, inc=1, device_id=row_device(k)[1], device_id_type=MESH)
    for k in range(1, n_seq):
        pl.semaphore_signal(
            barrier, inc=1, device_id={"seq": lax.rem(seq + k, n_seq)}, device_id_type=MESH
        )

    positions = [lengths[0] - DRAFT + offsets[0, t] for t in range(DRAFT)]
    limits = per_row(positions, (rows, 1), per_token)
    load_q.wait()
    latent_q = q_raw[:, :latent]
    rope_q = turned(q_raw[:, latent:].astype(jnp.float32), positions).astype(jnp.bfloat16)
    q_all[ctx, :, :latent] = latent_q
    q_all[ctx, :, latent:] = rope_q

    pl.semaphore_wait(barrier, n_out - 1 + n_seq - 1)

    step = jnp.where(ctx < n_ctx // 2, 1, n_ctx - 1)

    def peer(k):
        return lax.rem(ctx + k * step, n_ctx)

    def q_copy(k, slot):
        return pltpu.make_async_remote_copy(
            src_ref=q_all.at[ctx], dst_ref=q_all.at[slot],
            send_sem=q_send.at[k], recv_sem=q_recv.at[slot],
            device_id={"ctx": peer(k)}, device_id_type=MESH,
        )

    def part_copy(k, slot):
        return pltpu.make_async_remote_copy(
            src_ref=part_out.at[k], dst_ref=part_in.at[slot],
            send_sem=part_send.at[k], recv_sem=part_recv.at[slot],
            device_id={"ctx": peer(k)}, device_id_type=MESH,
        )

    def lse_copy(k, slot):
        return pltpu.make_async_remote_copy(
            src_ref=lse_out.at[k], dst_ref=lse_in.at[slot],
            send_sem=lse_send.at[k], recv_sem=lse_recv.at[slot],
            device_id={"ctx": peer(k)}, device_id_type=MESH,
        )

    for k in range(1, n_ctx):
        q_copy(k, ctx).start()

    load_keys.wait()
    load_uv.start()
    load_out.start()
    first_place = ctx * places
    batch = 2 if n_ctx % 2 == 0 else 1
    batch_limits = jnp.concatenate([limits] * batch, axis=0)

    def attend(block):
        scores = jnp.dot(block, keys[...], preferred_element_type=jnp.float32)
        place_of = first_place + lax.broadcasted_iota(jnp.int32, (1, places), 1)
        scores = jnp.where(place_of <= batch_limits, scores, NEGATIVE)
        maxima = jnp.max(scores, axis=1, keepdims=True)
        weights = jnp.exp2((scores - maxima) * (SCALE / LN2))
        totals = jnp.sum(weights, axis=1, keepdims=True)
        numerators = lax.dot_general(
            keys[:latent, :], weights.astype(jnp.bfloat16), (((1,), (1,)), ((), ())),
            preferred_element_type=jnp.float32,
        )
        return numerators.T / totals, maxima * SCALE + jnp.log(totals)

    diagonal = lax.broadcasted_iota(jnp.int32, (rows, rows), 0) == lax.broadcasted_iota(
        jnp.int32, (rows, rows), 1
    )

    def send_part(k, part, lse):
        part_out[k] = part.astype(jnp.bfloat16)
        as_row = jnp.sum(jnp.where(diagonal, lse, 0.0), axis=0, keepdims=True)
        lse_out[k] = jnp.broadcast_to(as_row, lse_out.shape[1:])
        part_copy(k, ctx).start()
        lse_copy(k, ctx).start()

    def remote_batch(j, carried):
        blocks = []
        for i in range(batch):
            owner = peer(j * batch + i)
            q_copy(j * batch + i, owner).wait_recv()
            blocks.append(q_all[owner])
        parts, lses = attend(jnp.concatenate(blocks, axis=0))
        for i in range(batch):
            mine = slice(i * rows, (i + 1) * rows)
            send_part(j * batch + i, parts[mine], lses[mine])
        return carried

    blocks = [q_all[ctx]]
    for k in range(1, batch):
        q_copy(k, peer(k)).wait_recv()
        blocks.append(q_all[peer(k)])
    parts, lses = attend(jnp.concatenate(blocks, axis=0))
    for k in range(1, batch):
        mine = slice(k * rows, (k + 1) * rows)
        send_part(k, parts[mine], lses[mine])
    own[...] = parts[:rows]
    own_lse = lses[:rows]

    lax.fori_loop(1, n_ctx // batch, remote_batch, 0)

    top = own_lse
    lses = []
    for k in range(1, n_ctx):
        slot = peer(k)
        lse_copy(k, slot).wait_recv()
        lse = jnp.sum(
            jnp.where(diagonal, lse_in[slot, 0:1, :], 0.0), axis=1, keepdims=True
        )
        lses.append(lse)
        top = jnp.maximum(top, lse)
    share = jnp.exp(own_lse - top)
    whole = share
    mixed = own[...] * share
    for k in range(1, n_ctx):
        slot = peer(k)
        part_copy(k, slot).wait_recv()
        share = jnp.exp(lses[k - 1] - top)
        whole = whole + share
        mixed = mixed + part_in[slot].astype(jnp.float32) * share
    mixed = mixed / whole
    for t in range(DRAFT):
        attended[t] = mixed[t * per_token : (t + 1) * per_token]

    load_uv.wait()
    vdim = w_uv.shape[2]
    for h in range(per_token):
        heads_all[seq, :, h * vdim : (h + 1) * vdim] = jnp.dot(
            attended[:, h, :].astype(jnp.bfloat16), w_uv[h], preferred_element_type=jnp.float32
        )

    def heads_copy(k, slot):
        return pltpu.make_async_remote_copy(
            src_ref=heads_all.at[seq], dst_ref=heads_all.at[slot],
            send_sem=heads_send.at[k], recv_sem=heads_recv.at[slot],
            device_id={"seq": lax.rem(seq + k, n_seq)}, device_id_type=MESH,
        )

    for k in range(1, n_seq):
        heads_copy(k, seq).start()
    columns = w_out.shape[1]
    n_parts = sums.shape[0]
    part_columns = columns // n_parts
    part_blocks = part_columns // LANES
    sums[...] = jnp.zeros_like(sums)
    load_out.wait()
    for k in range(1, n_seq):
        heads_copy(k, lax.rem(seq + k, n_seq)).wait_recv()
    tokens = jnp.concatenate([heads_all[s] for s in range(n_seq)], axis=0).astype(jnp.bfloat16)
    width = 2 * LANES if part_columns % (2 * LANES) == 0 else LANES

    def sums_copy(part, k, target, slot):
        return pltpu.make_async_remote_copy(
            src_ref=sums_out.at[part, target], dst_ref=sums_in.at[part, slot],
            send_sem=sums_send.at[part, k], recv_sem=sums_recv.at[part, slot],
            device_id=row_device(k)[1], device_id_type=MESH,
        )

    for part in range(n_parts):
        for first in range(0, part_columns, width):
            begin = part * part_columns + first
            product = jnp.dot(
                tokens, w_out[:, begin : begin + width], preferred_element_type=jnp.float32
            )
            for r in range(n_out):
                for i in range(width // LANES):
                    sums[part, r, first // LANES + i, :] = product[r, i * LANES : (i + 1) * LANES]
        for k in range(1, n_out):
            target = row_device(k)[0]
            sums_out[part, target] = sums[part, target].astype(jnp.bfloat16)
            sums_copy(part, k, target, place).start()
    for part in range(n_parts):
        result = sums[part, place]
        for k in range(1, n_out):
            slot = row_device(k)[0]
            sums_copy(part, k, slot, slot).wait_recv()
            result = result + sums_in[part, slot].astype(jnp.float32)
        for i in range(part_blocks):
            begin = part * part_columns + i * LANES
            out[:, begin : begin + LANES] = result[i : i + 1].astype(jnp.bfloat16)

    for k in range(1, n_ctx):
        q_copy(k, ctx).wait_send()
        part_copy(k, ctx).wait_send()
        lse_copy(k, ctx).wait_send()
    for k in range(1, n_seq):
        heads_copy(k, seq).wait_send()
    for part in range(n_parts):
        for k in range(1, n_out):
            sums_copy(part, k, row_device(k)[0], place).wait_send()


def per_device(sizes, queries, cache, lengths, offsets, w_uv, w_out):
    n_ctx, n_seq, n_head = sizes
    n_out = n_ctx * n_head
    heads, entries = queries.shape[2:]
    rows = DRAFT * heads
    places = cache.shape[1]
    latent, vdim = w_uv.shape[1:]
    columns = w_out.shape[1]
    n_blocks = columns // LANES
    n_parts = 2 if n_blocks % 2 == 0 else 1
    padded = -(-n_blocks // n_parts // 16) * 16
    sixteen, full = jnp.bfloat16, jnp.float32
    dma = pltpu.SemaphoreType.DMA
    smem = pl.BlockSpec(memory_space=pltpu.SMEM)
    anywhere = pl.BlockSpec(memory_space=pl.ANY)
    return pl.pallas_call(
        functools.partial(kernel, sizes),
        out_shape=jax.ShapeDtypeStruct((1, columns), sixteen),
        in_specs=[smem, smem, anywhere, anywhere, anywhere, anywhere],
        out_specs=pl.BlockSpec(memory_space=pltpu.VMEM),
        scratch_shapes=[
            pltpu.VMEM((rows, entries), sixteen),
            pltpu.VMEM((n_ctx, rows, entries), sixteen),
            pltpu.VMEM((entries, places), sixteen),
            pltpu.VMEM(w_uv.shape, sixteen),
            pltpu.VMEM(w_out.shape, sixteen),
            pltpu.VMEM((rows, latent), full),
            pltpu.VMEM((n_ctx, rows, latent), sixteen),
            pltpu.VMEM((n_ctx, rows, latent), sixteen),
            pltpu.VMEM((n_ctx, 8, rows), full),
            pltpu.VMEM((n_ctx, 8, rows), full),
            pltpu.VMEM((DRAFT, heads, latent), full),
            pltpu.VMEM((n_seq, DRAFT, heads * vdim), full),
            pltpu.VMEM((n_parts, n_out, padded, LANES), full),
            pltpu.VMEM((n_parts, n_out, padded, LANES), sixteen),
            pltpu.VMEM((n_parts, n_out, padded, LANES), sixteen),
            dma((4,)),
            dma((n_ctx,)), dma((n_ctx,)),
            dma((n_ctx,)), dma((n_ctx,)),
            dma((n_ctx,)), dma((n_ctx,)),
            dma((n_seq,)), dma((n_seq,)),
            dma((n_parts, n_out)), dma((n_parts, n_out)),
        ],
        compiler_params=pltpu.CompilerParams(
            collective_id=0, has_side_effects=True, vmem_limit_bytes=60 * 2**20
        ),
        name="latent_attention",
    )(
        lengths,
        offsets,
        queries.reshape(rows, entries),
        jnp.swapaxes(cache[0], 0, 1),
        w_uv,
        w_out,
    )


def solution(mesh):
    sizes = (mesh.shape["ctx"], mesh.shape["seq"], mesh.shape["head"])
    in_specs = (
        P(("groups", "seq"), None, ("ctx", "head"), None),
        P(("groups", "seq"), "ctx", None),
        P(("groups", "seq")),
        P(("groups", "seq"), None),
        P(("ctx", "head"), None, None),
        P(("ctx", "head"), "seq"),
    )
    out_specs = P(("groups", "ctx", "head"), "seq")
    return jax.shard_map(
        functools.partial(per_device, sizes),
        mesh=mesh, in_specs=in_specs, out_specs=out_specs, check_vma=False,
    )
```

```python
import functools
import math

import jax
import jax.numpy as jnp
from jax import lax
from jax.experimental import pallas as pl
from jax.experimental.pallas import tpu as pltpu
from jax.sharding import PartitionSpec as P

ROPE = 64
NOPE = 128
DRAFT = 4
LANES = 128
THETA = 10000.0
NEGATIVE = -1e30
SCALE = (NOPE + ROPE) ** -0.5
LN2 = math.log(2.0)
TURN = 2.0 * math.pi
TURN_HIGH = 6.28125
TURN_MID = math.floor((TURN - TURN_HIGH) * 2**19) / 2**19
TURN_LOW = TURN - TURN_HIGH - TURN_MID
MESH = pl.DeviceIdType.MESH


def sine_cosine(angle):
    turns = jnp.floor(angle * (1.0 / TURN) + 0.5)
    r = ((angle - turns * TURN_HIGH) - turns * TURN_MID) - turns * TURN_LOW
    square = r * r
    sine = jnp.zeros_like(r)
    cosine = jnp.zeros_like(r)
    for i in range(9, -1, -1):
        sign = -1.0 if i % 2 else 1.0
        cosine = cosine * square + sign / math.factorial(2 * i)
        sine = sine * square + sign / math.factorial(2 * i + 1)
    return sine * r, cosine


def per_row(scalars, shape, per_token):
    row = lax.broadcasted_iota(jnp.int32, shape, 0)
    column = jnp.full(shape, scalars[-1])
    for t in range(len(scalars) - 2, -1, -1):
        column = jnp.where(row < (t + 1) * per_token, scalars[t], column)
    return column


def turned(rope, positions):
    rows = rope.shape[0]
    half = ROPE // 2
    lane = lax.broadcasted_iota(jnp.int32, (1, ROPE), 1)
    frequency = jnp.zeros((1, ROPE), jnp.float32)
    for i in range(half):
        frequency = jnp.where(lane % half == i, THETA ** (-2.0 * i / ROPE), frequency)
    position = per_row(positions, (rows, ROPE), rows // DRAFT).astype(jnp.float32)
    sine, cosine = sine_cosine(position * frequency)
    swapped = jnp.concatenate([rope[:, half:], rope[:, :half]], axis=1)
    return rope * cosine + jnp.where(lane < half, -swapped, swapped) * sine


def kernel(
    sizes,
    lengths, offsets, q_hbm, keys_hbm, w_uv_hbm, w_out_hbm,
    out,
    q_raw, q_all, keys, w_uv, w_out, own, part_out, part_in, lse_out, lse_in,
    attended, heads_all, sums, sums_out, sums_in,
    load_sem, q_send, q_recv, part_send, part_recv, lse_send, lse_recv,
    heads_send, heads_recv, sums_send, sums_recv,
):
    n_ctx, n_seq, n_head = sizes
    ctx, seq, head = lax.axis_index("ctx"), lax.axis_index("seq"), lax.axis_index("head")
    rows, entries = q_raw.shape
    latent, places = own.shape[1], keys.shape[1]
    per_token = rows // DRAFT
    n_out = n_ctx * n_head
    place = ctx * n_head + head

    load_q = pltpu.make_async_copy(q_hbm, q_raw, load_sem.at[0])
    load_keys = pltpu.make_async_copy(keys_hbm, keys, load_sem.at[1])
    load_uv = pltpu.make_async_copy(w_uv_hbm, w_uv, load_sem.at[2])
    load_out = pltpu.make_async_copy(w_out_hbm, w_out, load_sem.at[3])
    load_q.start()
    load_keys.start()

    def row_device(k):
        other = lax.rem(place + k, n_out)
        return other, {"ctx": other // n_head, "head": lax.rem(other, n_head)}

    barrier = pltpu.get_barrier_semaphore()
    for k in range(1, n_out):
        pl.semaphore_signal(barrier, inc=1, device_id=row_device(k)[1], device_id_type=MESH)
    for k in range(1, n_seq):
        pl.semaphore_signal(
            barrier, inc=1, device_id={"seq": lax.rem(seq + k, n_seq)}, device_id_type=MESH
        )

    positions = [lengths[0] - DRAFT + offsets[0, t] for t in range(DRAFT)]
    limits = per_row(positions, (rows, 1), per_token)
    load_q.wait()
    latent_q = q_raw[:, :latent]
    rope_q = turned(q_raw[:, latent:].astype(jnp.float32), positions).astype(jnp.bfloat16)
    q_all[ctx, :, :latent] = latent_q
    q_all[ctx, :, latent:] = rope_q

    pl.semaphore_wait(barrier, n_out - 1 + n_seq - 1)

    toward = jnp.where(ctx < n_ctx // 2, 1, -1)
    shorter = jnp.minimum(ctx, n_ctx - 1 - ctx)

    def peer(k):
        near = jnp.where(lax.rem(k, 2) == 1, (k + 1) // 2, -(k // 2))
        return ctx + toward * jnp.where(k <= 2 * shorter, near, k - shorter)

    def q_copy(owner, side, send):
        return pltpu.make_async_remote_copy(
            src_ref=q_all.at[owner], dst_ref=q_all.at[owner],
            send_sem=q_send.at[send], recv_sem=q_recv.at[owner],
            device_id={"ctx": ctx + side}, device_id_type=MESH,
        )

    has_left, has_right = ctx > 0, ctx < n_ctx - 1

    @pl.when(has_right)
    def _():
        q_copy(ctx, 1, ctx).start()

    @pl.when(has_left)
    def _():
        q_copy(ctx, -1, n_ctx).start()

    def pass_on(distance):
        @pl.when(ctx - distance >= 0)
        def _():
            q_copy(ctx - distance, -1, 0).wait_recv()

            @pl.when(has_right)
            def _():
                q_copy(ctx - distance, 1, ctx - distance).start()

        @pl.when(ctx + distance < n_ctx)
        def _():
            q_copy(ctx + distance, 1, 0).wait_recv()

            @pl.when(has_left)
            def _():
                q_copy(ctx + distance, -1, ctx + distance).start()

    def part_copy(k, slot):
        return pltpu.make_async_remote_copy(
            src_ref=part_out.at[k], dst_ref=part_in.at[slot],
            send_sem=part_send.at[k], recv_sem=part_recv.at[slot],
            device_id={"ctx": peer(k)}, device_id_type=MESH,
        )

    def lse_copy(k, slot):
        return pltpu.make_async_remote_copy(
            src_ref=lse_out.at[k], dst_ref=lse_in.at[slot],
            send_sem=lse_send.at[k], recv_sem=lse_recv.at[slot],
            device_id={"ctx": peer(k)}, device_id_type=MESH,
        )

    load_keys.wait()
    load_uv.start()
    load_out.start()
    first_place = ctx * places

    def attend(block):
        scores = jnp.dot(block, keys[...], preferred_element_type=jnp.float32)
        place_of = first_place + lax.broadcasted_iota(jnp.int32, (1, places), 1)
        scores = jnp.where(place_of <= limits, scores, NEGATIVE)
        maxima = jnp.max(scores, axis=1, keepdims=True)
        weights = jnp.exp2((scores - maxima) * (SCALE / LN2))
        totals = jnp.sum(weights, axis=1, keepdims=True)
        numerators = lax.dot_general(
            keys[:latent, :], weights.astype(jnp.bfloat16), (((1,), (1,)), ((), ())),
            preferred_element_type=jnp.float32,
        )
        return numerators.T / totals, maxima * SCALE + jnp.log(totals)

    diagonal = lax.broadcasted_iota(jnp.int32, (rows, rows), 0) == lax.broadcasted_iota(
        jnp.int32, (rows, rows), 1
    )

    def send_part(k, part, lse):
        part_out[k] = part.astype(jnp.bfloat16)
        as_row = jnp.sum(jnp.where(diagonal, lse, 0.0), axis=0, keepdims=True)
        lse_out[k] = jnp.broadcast_to(as_row, lse_out.shape[1:])
        part_copy(k, ctx).start()
        lse_copy(k, ctx).start()

    def remote_block(k, carried):
        pass_on(k)
        send_part(k, *attend(q_all[peer(k)]))
        return carried

    own_part, own_lse = attend(q_all[ctx])
    own[...] = own_part
    lax.fori_loop(1, n_ctx, remote_block, 0)

    top = own_lse
    lses = []
    for k in range(1, n_ctx):
        slot = peer(k)
        lse_copy(k, slot).wait_recv()
        lse = jnp.sum(
            jnp.where(diagonal, lse_in[slot, 0:1, :], 0.0), axis=1, keepdims=True
        )
        lses.append(lse)
        top = jnp.maximum(top, lse)
    share = jnp.exp(own_lse - top)
    whole = share
    mixed = own[...] * share
    for k in range(1, n_ctx):
        slot = peer(k)
        part_copy(k, slot).wait_recv()
        share = jnp.exp(lses[k - 1] - top)
        whole = whole + share
        mixed = mixed + part_in[slot].astype(jnp.float32) * share
    mixed = mixed / whole
    for t in range(DRAFT):
        attended[t] = mixed[t * per_token : (t + 1) * per_token]

    load_uv.wait()
    vdim = w_uv.shape[2]
    for h in range(per_token):
        heads_all[seq, :, h * vdim : (h + 1) * vdim] = jnp.dot(
            attended[:, h, :].astype(jnp.bfloat16), w_uv[h], preferred_element_type=jnp.float32
        )

    def heads_copy(k, slot):
        return pltpu.make_async_remote_copy(
            src_ref=heads_all.at[seq], dst_ref=heads_all.at[slot],
            send_sem=heads_send.at[k], recv_sem=heads_recv.at[slot],
            device_id={"seq": lax.rem(seq + k, n_seq)}, device_id_type=MESH,
        )

    for k in range(1, n_seq):
        heads_copy(k, seq).start()
    columns = w_out.shape[1]
    n_parts = sums.shape[0]
    part_columns = columns // n_parts
    part_blocks = part_columns // LANES
    sums[...] = jnp.zeros_like(sums)
    load_out.wait()
    for k in range(1, n_seq):
        heads_copy(k, lax.rem(seq + k, n_seq)).wait_recv()
    tokens = jnp.concatenate([heads_all[s] for s in range(n_seq)], axis=0).astype(jnp.bfloat16)
    width = 2 * LANES if part_columns % (2 * LANES) == 0 else LANES

    def sums_copy(part, k, target, slot):
        return pltpu.make_async_remote_copy(
            src_ref=sums_out.at[part, target], dst_ref=sums_in.at[part, slot],
            send_sem=sums_send.at[part, k], recv_sem=sums_recv.at[part, slot],
            device_id=row_device(k)[1], device_id_type=MESH,
        )

    for part in range(n_parts):
        for first in range(0, part_columns, width):
            begin = part * part_columns + first
            product = jnp.dot(
                tokens, w_out[:, begin : begin + width], preferred_element_type=jnp.float32
            )
            for r in range(n_out):
                for i in range(width // LANES):
                    sums[part, r, first // LANES + i, :] = product[r, i * LANES : (i + 1) * LANES]
        for k in range(1, n_out):
            target = row_device(k)[0]
            sums_out[part, target] = sums[part, target].astype(jnp.bfloat16)
            sums_copy(part, k, target, place).start()
    for part in range(n_parts):
        result = sums[part, place]
        for k in range(1, n_out):
            slot = row_device(k)[0]
            sums_copy(part, k, slot, slot).wait_recv()
            result = result + sums_in[part, slot].astype(jnp.float32)
        for i in range(part_blocks):
            begin = part * part_columns + i * LANES
            out[:, begin : begin + LANES] = result[i : i + 1].astype(jnp.bfloat16)

    @pl.when(has_right)
    def _():
        q_copy(ctx, 1, ctx).wait_send()

    @pl.when(has_left)
    def _():
        q_copy(ctx, -1, n_ctx).wait_send()

    for k in range(1, n_ctx):
        @pl.when((ctx - k >= 0) & has_right)
        def _():
            q_copy(ctx - k, 1, ctx - k).wait_send()

        @pl.when((ctx + k < n_ctx) & has_left)
        def _():
            q_copy(ctx + k, -1, ctx + k).wait_send()

        part_copy(k, ctx).wait_send()
        lse_copy(k, ctx).wait_send()
    for k in range(1, n_seq):
        heads_copy(k, seq).wait_send()
    for part in range(n_parts):
        for k in range(1, n_out):
            sums_copy(part, k, row_device(k)[0], place).wait_send()


def per_device(sizes, queries, cache, lengths, offsets, w_uv, w_out):
    n_ctx, n_seq, n_head = sizes
    n_out = n_ctx * n_head
    heads, entries = queries.shape[2:]
    rows = DRAFT * heads
    places = cache.shape[1]
    latent, vdim = w_uv.shape[1:]
    columns = w_out.shape[1]
    n_blocks = columns // LANES
    n_parts = 2 if n_blocks % 2 == 0 else 1
    padded = -(-n_blocks // n_parts // 16) * 16
    sixteen, full = jnp.bfloat16, jnp.float32
    dma = pltpu.SemaphoreType.DMA
    smem = pl.BlockSpec(memory_space=pltpu.SMEM)
    anywhere = pl.BlockSpec(memory_space=pl.ANY)
    return pl.pallas_call(
        functools.partial(kernel, sizes),
        out_shape=jax.ShapeDtypeStruct((1, columns), sixteen),
        in_specs=[smem, smem, anywhere, anywhere, anywhere, anywhere],
        out_specs=pl.BlockSpec(memory_space=pltpu.VMEM),
        scratch_shapes=[
            pltpu.VMEM((rows, entries), sixteen),
            pltpu.VMEM((n_ctx, rows, entries), sixteen),
            pltpu.VMEM((entries, places), sixteen),
            pltpu.VMEM(w_uv.shape, sixteen),
            pltpu.VMEM(w_out.shape, sixteen),
            pltpu.VMEM((rows, latent), full),
            pltpu.VMEM((n_ctx, rows, latent), sixteen),
            pltpu.VMEM((n_ctx, rows, latent), sixteen),
            pltpu.VMEM((n_ctx, 8, rows), full),
            pltpu.VMEM((n_ctx, 8, rows), full),
            pltpu.VMEM((DRAFT, heads, latent), full),
            pltpu.VMEM((n_seq, DRAFT, heads * vdim), full),
            pltpu.VMEM((n_parts, n_out, padded, LANES), full),
            pltpu.VMEM((n_parts, n_out, padded, LANES), sixteen),
            pltpu.VMEM((n_parts, n_out, padded, LANES), sixteen),
            dma((4,)),
            dma((n_ctx + 1,)), dma((n_ctx,)),
            dma((n_ctx,)), dma((n_ctx,)),
            dma((n_ctx,)), dma((n_ctx,)),
            dma((n_seq,)), dma((n_seq,)),
            dma((n_parts, n_out)), dma((n_parts, n_out)),
        ],
        compiler_params=pltpu.CompilerParams(
            collective_id=0, has_side_effects=True, vmem_limit_bytes=60 * 2**20
        ),
        name="latent_attention",
    )(
        lengths,
        offsets,
        queries.reshape(rows, entries),
        jnp.swapaxes(cache[0], 0, 1),
        w_uv,
        w_out,
    )


def solution(mesh):
    sizes = (mesh.shape["ctx"], mesh.shape["seq"], mesh.shape["head"])
    in_specs = (
        P(("groups", "seq"), None, ("ctx", "head"), None),
        P(("groups", "seq"), "ctx", None),
        P(("groups", "seq")),
        P(("groups", "seq"), None),
        P(("ctx", "head"), None, None),
        P(("ctx", "head"), "seq"),
    )
    out_specs = P(("groups", "ctx", "head"), "seq")
    return jax.shard_map(
        functools.partial(per_device, sizes),
        mesh=mesh, in_specs=in_specs, out_specs=out_specs, check_vma=False,
    )
```

```python
import functools
import math

import jax
import jax.numpy as jnp
from jax import lax
from jax.experimental import pallas as pl
from jax.experimental.pallas import tpu as pltpu
from jax.sharding import PartitionSpec as P

ROPE = 64
NOPE = 128
DRAFT = 4
LANES = 128
THETA = 10000.0
NEGATIVE = -1e30
SCALE = (NOPE + ROPE) ** -0.5
LN2 = math.log(2.0)
TURN = 2.0 * math.pi
TURN_HIGH = 6.28125
TURN_MID = math.floor((TURN - TURN_HIGH) * 2**19) / 2**19
TURN_LOW = TURN - TURN_HIGH - TURN_MID
MESH = pl.DeviceIdType.MESH


def sine_cosine(angle):
    turns = jnp.floor(angle * (1.0 / TURN) + 0.5)
    r = ((angle - turns * TURN_HIGH) - turns * TURN_MID) - turns * TURN_LOW
    square = r * r
    sine = jnp.zeros_like(r)
    cosine = jnp.zeros_like(r)
    for i in range(9, -1, -1):
        sign = -1.0 if i % 2 else 1.0
        cosine = cosine * square + sign / math.factorial(2 * i)
        sine = sine * square + sign / math.factorial(2 * i + 1)
    return sine * r, cosine


def per_row(scalars, shape, per_token):
    row = lax.broadcasted_iota(jnp.int32, shape, 0)
    column = jnp.full(shape, scalars[-1])
    for t in range(len(scalars) - 2, -1, -1):
        column = jnp.where(row < (t + 1) * per_token, scalars[t], column)
    return column


def turned(rope, positions):
    rows = rope.shape[0]
    half = ROPE // 2
    lane = lax.broadcasted_iota(jnp.int32, (1, ROPE), 1)
    frequency = jnp.zeros((1, ROPE), jnp.float32)
    for i in range(half):
        frequency = jnp.where(lane % half == i, THETA ** (-2.0 * i / ROPE), frequency)
    position = per_row(positions, (rows, ROPE), rows // DRAFT).astype(jnp.float32)
    sine, cosine = sine_cosine(position * frequency)
    swapped = jnp.concatenate([rope[:, half:], rope[:, :half]], axis=1)
    return rope * cosine + jnp.where(lane < half, -swapped, swapped) * sine


def kernel(
    sizes,
    lengths, offsets, q_hbm, keys_hbm, w_uv_hbm, w_out_hbm,
    out,
    q_raw, q_all, keys, w_uv, w_out, own, part_out, part_in, lse_out, lse_in,
    attended, heads_all, sums, sums_out, sums_in,
    load_sem, keys_sem, uv_sem, out_sem, q_send, q_recv, part_send, part_recv, lse_send, lse_recv,
    heads_send, heads_recv, sums_send, sums_recv,
):
    n_ctx, n_seq, n_head = sizes
    ctx, seq, head = lax.axis_index("ctx"), lax.axis_index("seq"), lax.axis_index("head")
    rows, entries = q_raw.shape
    latent, places = own.shape[1], keys.shape[1]
    per_token = rows // DRAFT
    n_out = n_ctx * n_head
    place = ctx * n_head + head

    load_q = pltpu.make_async_copy(q_hbm, q_raw, load_sem.at[0])

    def loads(source, target, sems, count):
        size = source.shape[0] // count
        return [
            pltpu.make_async_copy(
                source.at[pl.ds(i * size, size)], target.at[pl.ds(i * size, size)], sems.at[i]
            )
            for i in range(count)
        ]

    load_keys = loads(keys_hbm, keys, keys_sem, keys_sem.shape[0])
    load_uv = loads(w_uv_hbm, w_uv, uv_sem, uv_sem.shape[0])
    load_out = loads(w_out_hbm, w_out, out_sem, out_sem.shape[0])
    load_q.start()
    for copy in load_keys + load_uv + load_out:
        copy.start()

    def row_device(k):
        other = lax.rem(place + k, n_out)
        return other, {"ctx": other // n_head, "head": lax.rem(other, n_head)}

    barrier = pltpu.get_barrier_semaphore()
    for k in range(1, n_out):
        pl.semaphore_signal(barrier, inc=1, device_id=row_device(k)[1], device_id_type=MESH)
    for k in range(1, n_seq):
        pl.semaphore_signal(
            barrier, inc=1, device_id={"seq": lax.rem(seq + k, n_seq)}, device_id_type=MESH
        )

    positions = [lengths[0] - DRAFT + offsets[0, t] for t in range(DRAFT)]
    limits = per_row(positions, (rows, 1), per_token)
    load_q.wait()
    latent_q = q_raw[:, :latent]
    rope_q = turned(q_raw[:, latent:].astype(jnp.float32), positions).astype(jnp.bfloat16)
    q_all[ctx, :, :latent] = latent_q
    q_all[ctx, :, latent:] = rope_q

    pl.semaphore_wait(barrier, n_out - 1 + n_seq - 1)

    toward = jnp.where(ctx < n_ctx // 2, 1, -1)
    shorter = jnp.minimum(ctx, n_ctx - 1 - ctx)

    def peer(k):
        near = jnp.where(lax.rem(k, 2) == 1, (k + 1) // 2, -(k // 2))
        return ctx + toward * jnp.where(k <= 2 * shorter, near, k - shorter)

    def q_copy(owner, side, send):
        return pltpu.make_async_remote_copy(
            src_ref=q_all.at[owner], dst_ref=q_all.at[owner],
            send_sem=q_send.at[send], recv_sem=q_recv.at[owner],
            device_id={"ctx": ctx + side}, device_id_type=MESH,
        )

    has_left, has_right = ctx > 0, ctx < n_ctx - 1

    @pl.when(has_right)
    def _():
        q_copy(ctx, 1, ctx).start()

    @pl.when(has_left)
    def _():
        q_copy(ctx, -1, n_ctx).start()

    def pass_on(distance):
        @pl.when(ctx - distance >= 0)
        def _():
            q_copy(ctx - distance, -1, 0).wait_recv()

            @pl.when(has_right)
            def _():
                q_copy(ctx - distance, 1, ctx - distance).start()

        @pl.when(ctx + distance < n_ctx)
        def _():
            q_copy(ctx + distance, 1, 0).wait_recv()

            @pl.when(has_left)
            def _():
                q_copy(ctx + distance, -1, ctx + distance).start()

    def part_copy(k, slot):
        return pltpu.make_async_remote_copy(
            src_ref=part_out.at[k], dst_ref=part_in.at[slot],
            send_sem=part_send.at[k], recv_sem=part_recv.at[slot],
            device_id={"ctx": peer(k)}, device_id_type=MESH,
        )

    def lse_copy(k, slot):
        return pltpu.make_async_remote_copy(
            src_ref=lse_out.at[k], dst_ref=lse_in.at[slot],
            send_sem=lse_send.at[k], recv_sem=lse_recv.at[slot],
            device_id={"ctx": peer(k)}, device_id_type=MESH,
        )

    for copy in load_keys:
        copy.wait()
    first_place = ctx * places

    def attend(block):
        scores = jnp.dot(block, keys[...], preferred_element_type=jnp.float32)
        place_of = first_place + lax.broadcasted_iota(jnp.int32, (1, places), 1)
        scores = jnp.where(place_of <= limits, scores, NEGATIVE)
        maxima = jnp.max(scores, axis=1, keepdims=True)
        weights = jnp.exp2((scores - maxima) * (SCALE / LN2))
        totals = jnp.sum(weights, axis=1, keepdims=True)
        numerators = lax.dot_general(
            keys[:latent, :], weights.astype(jnp.bfloat16), (((1,), (1,)), ((), ())),
            preferred_element_type=jnp.float32,
        )
        return numerators.T / totals, maxima * SCALE + jnp.log(totals)

    diagonal = lax.broadcasted_iota(jnp.int32, (rows, rows), 0) == lax.broadcasted_iota(
        jnp.int32, (rows, rows), 1
    )

    def send_part(k, part, lse):
        part_out[k] = part.astype(jnp.bfloat16)
        as_row = jnp.sum(jnp.where(diagonal, lse, 0.0), axis=0, keepdims=True)
        lse_out[k] = jnp.broadcast_to(as_row, lse_out.shape[1:])
        part_copy(k, ctx).start()
        lse_copy(k, ctx).start()

    def remote_block(k, carried):
        pass_on(k)
        send_part(k, *attend(q_all[peer(k)]))
        return carried

    own_part, own_lse = attend(q_all[ctx])
    own[...] = own_part
    lax.fori_loop(1, n_ctx, remote_block, 0)

    top = own_lse
    lses = []
    for k in range(1, n_ctx):
        slot = peer(k)
        lse_copy(k, slot).wait_recv()
        lse = jnp.sum(
            jnp.where(diagonal, lse_in[slot, 0:1, :], 0.0), axis=1, keepdims=True
        )
        lses.append(lse)
        top = jnp.maximum(top, lse)
    share = jnp.exp(own_lse - top)
    whole = share
    mixed = own[...] * share
    for k in range(1, n_ctx):
        slot = peer(k)
        part_copy(k, slot).wait_recv()
        share = jnp.exp(lses[k - 1] - top)
        whole = whole + share
        mixed = mixed + part_in[slot].astype(jnp.float32) * share
    mixed = mixed / whole
    for t in range(DRAFT):
        attended[t] = mixed[t * per_token : (t + 1) * per_token]

    for copy in load_uv:
        copy.wait()
    vdim = w_uv.shape[2]
    for h in range(per_token):
        heads_all[seq, :, h * vdim : (h + 1) * vdim] = jnp.dot(
            attended[:, h, :].astype(jnp.bfloat16), w_uv[h], preferred_element_type=jnp.float32
        )

    def heads_copy(k, slot):
        return pltpu.make_async_remote_copy(
            src_ref=heads_all.at[seq], dst_ref=heads_all.at[slot],
            send_sem=heads_send.at[k], recv_sem=heads_recv.at[slot],
            device_id={"seq": lax.rem(seq + k, n_seq)}, device_id_type=MESH,
        )

    for k in range(1, n_seq):
        heads_copy(k, seq).start()
    columns = w_out.shape[1]
    n_parts = sums.shape[0]
    part_columns = columns // n_parts
    part_blocks = part_columns // LANES
    sums[...] = jnp.zeros_like(sums)
    for copy in load_out:
        copy.wait()
    for k in range(1, n_seq):
        heads_copy(k, lax.rem(seq + k, n_seq)).wait_recv()
    tokens = jnp.concatenate([heads_all[s] for s in range(n_seq)], axis=0).astype(jnp.bfloat16)
    width = 2 * LANES if part_columns % (2 * LANES) == 0 else LANES

    def sums_copy(part, k, target, slot):
        return pltpu.make_async_remote_copy(
            src_ref=sums_out.at[part, target], dst_ref=sums_in.at[part, slot],
            send_sem=sums_send.at[part, k], recv_sem=sums_recv.at[part, slot],
            device_id=row_device(k)[1], device_id_type=MESH,
        )

    for part in range(n_parts):
        for first in range(0, part_columns, width):
            begin = part * part_columns + first
            product = jnp.dot(
                tokens, w_out[:, begin : begin + width], preferred_element_type=jnp.float32
            )
            for r in range(n_out):
                for i in range(width // LANES):
                    sums[part, r, first // LANES + i, :] = product[r, i * LANES : (i + 1) * LANES]
        for k in range(1, n_out):
            target = row_device(k)[0]
            sums_out[part, target] = sums[part, target].astype(jnp.bfloat16)
            sums_copy(part, k, target, place).start()
    for part in range(n_parts):
        result = sums[part, place]
        for k in range(1, n_out):
            slot = row_device(k)[0]
            sums_copy(part, k, slot, slot).wait_recv()
            result = result + sums_in[part, slot].astype(jnp.float32)
        for i in range(part_blocks):
            begin = part * part_columns + i * LANES
            out[:, begin : begin + LANES] = result[i : i + 1].astype(jnp.bfloat16)

    @pl.when(has_right)
    def _():
        q_copy(ctx, 1, ctx).wait_send()

    @pl.when(has_left)
    def _():
        q_copy(ctx, -1, n_ctx).wait_send()

    for k in range(1, n_ctx):
        @pl.when((ctx - k >= 0) & has_right)
        def _():
            q_copy(ctx - k, 1, ctx - k).wait_send()

        @pl.when((ctx + k < n_ctx) & has_left)
        def _():
            q_copy(ctx + k, -1, ctx + k).wait_send()

        part_copy(k, ctx).wait_send()
        lse_copy(k, ctx).wait_send()
    for k in range(1, n_seq):
        heads_copy(k, seq).wait_send()
    for part in range(n_parts):
        for k in range(1, n_out):
            sums_copy(part, k, row_device(k)[0], place).wait_send()


def per_device(sizes, queries, cache, lengths, offsets, w_uv, w_out):
    n_ctx, n_seq, n_head = sizes
    n_out = n_ctx * n_head
    heads, entries = queries.shape[2:]
    rows = DRAFT * heads
    places = cache.shape[1]
    latent, vdim = w_uv.shape[1:]
    columns = w_out.shape[1]
    n_blocks = columns // LANES
    n_parts = 2 if n_blocks % 2 == 0 else 1
    padded = -(-n_blocks // n_parts // 16) * 16
    sixteen, full = jnp.bfloat16, jnp.float32
    dma = pltpu.SemaphoreType.DMA
    smem = pl.BlockSpec(memory_space=pltpu.SMEM)
    anywhere = pl.BlockSpec(memory_space=pl.ANY)
    return pl.pallas_call(
        functools.partial(kernel, sizes),
        out_shape=jax.ShapeDtypeStruct((1, columns), sixteen),
        in_specs=[smem, smem, anywhere, anywhere, anywhere, anywhere],
        out_specs=pl.BlockSpec(memory_space=pltpu.VMEM),
        scratch_shapes=[
            pltpu.VMEM((rows, entries), sixteen),
            pltpu.VMEM((n_ctx, rows, entries), sixteen),
            pltpu.VMEM((entries, places), sixteen),
            pltpu.VMEM(w_uv.shape, sixteen),
            pltpu.VMEM(w_out.shape, sixteen),
            pltpu.VMEM((rows, latent), full),
            pltpu.VMEM((n_ctx, rows, latent), sixteen),
            pltpu.VMEM((n_ctx, rows, latent), sixteen),
            pltpu.VMEM((n_ctx, 8, rows), full),
            pltpu.VMEM((n_ctx, 8, rows), full),
            pltpu.VMEM((DRAFT, heads, latent), full),
            pltpu.VMEM((n_seq, DRAFT, heads * vdim), full),
            pltpu.VMEM((n_parts, n_out, padded, LANES), full),
            pltpu.VMEM((n_parts, n_out, padded, LANES), sixteen),
            pltpu.VMEM((n_parts, n_out, padded, LANES), sixteen),
            dma((1,)), dma((entries // ROPE,)), dma((4,)), dma((16,)),
            dma((n_ctx + 1,)), dma((n_ctx,)),
            dma((n_ctx,)), dma((n_ctx,)),
            dma((n_ctx,)), dma((n_ctx,)),
            dma((n_seq,)), dma((n_seq,)),
            dma((n_parts, n_out)), dma((n_parts, n_out)),
        ],
        compiler_params=pltpu.CompilerParams(
            collective_id=0, has_side_effects=True, vmem_limit_bytes=60 * 2**20
        ),
        name="latent_attention",
    )(
        lengths,
        offsets,
        queries.reshape(rows, entries),
        jnp.swapaxes(cache[0], 0, 1),
        w_uv,
        w_out,
    )


def solution(mesh):
    sizes = (mesh.shape["ctx"], mesh.shape["seq"], mesh.shape["head"])
    in_specs = (
        P(("groups", "seq"), None, ("ctx", "head"), None),
        P(("groups", "seq"), "ctx", None),
        P(("groups", "seq")),
        P(("groups", "seq"), None),
        P(("ctx", "head"), None, None),
        P(("ctx", "head"), "seq"),
    )
    out_specs = P(("groups", "ctx", "head"), "seq")
    return jax.shard_map(
        functools.partial(per_device, sizes),
        mesh=mesh, in_specs=in_specs, out_specs=out_specs, check_vma=False,
    )
```

```python
import functools
import math

import jax
import jax.numpy as jnp
from jax import lax
from jax.experimental import pallas as pl
from jax.experimental.pallas import tpu as pltpu
from jax.sharding import PartitionSpec as P

ROPE = 64
NOPE = 128
DRAFT = 4
LANES = 128
THETA = 10000.0
NEGATIVE = -1e30
SCALE = (NOPE + ROPE) ** -0.5
LN2 = math.log(2.0)
TURN = 2.0 * math.pi
TURN_HIGH = 6.28125
TURN_MID = math.floor((TURN - TURN_HIGH) * 2**19) / 2**19
TURN_LOW = TURN - TURN_HIGH - TURN_MID
MESH = pl.DeviceIdType.MESH


def sine_cosine(angle):
    turns = jnp.floor(angle * (1.0 / TURN) + 0.5)
    r = ((angle - turns * TURN_HIGH) - turns * TURN_MID) - turns * TURN_LOW
    square = r * r
    sine = jnp.zeros_like(r)
    cosine = jnp.zeros_like(r)
    for i in range(9, -1, -1):
        sign = -1.0 if i % 2 else 1.0
        cosine = cosine * square + sign / math.factorial(2 * i)
        sine = sine * square + sign / math.factorial(2 * i + 1)
    return sine * r, cosine


def per_row(scalars, shape, per_token):
    row = lax.broadcasted_iota(jnp.int32, shape, 0)
    column = jnp.full(shape, scalars[-1])
    for t in range(len(scalars) - 2, -1, -1):
        column = jnp.where(row < (t + 1) * per_token, scalars[t], column)
    return column


def turned(rope, positions):
    rows = rope.shape[0]
    half = ROPE // 2
    lane = lax.broadcasted_iota(jnp.int32, (1, ROPE), 1)
    frequency = jnp.zeros((1, ROPE), jnp.float32)
    for i in range(half):
        frequency = jnp.where(lane % half == i, THETA ** (-2.0 * i / ROPE), frequency)
    position = per_row(positions, (rows, ROPE), rows // DRAFT).astype(jnp.float32)
    sine, cosine = sine_cosine(position * frequency)
    swapped = jnp.concatenate([rope[:, half:], rope[:, :half]], axis=1)
    return rope * cosine + jnp.where(lane < half, -swapped, swapped) * sine


def kernel(
    sizes,
    lengths, offsets, q_hbm, keys_hbm, w_uv_hbm, w_out_hbm,
    out,
    q_raw, q_all, keys, scores, w_uv, w_out, own, part_out, part_in, lse_out, lse_in,
    attended, heads_all, sums, sums_out, sums_in,
    load_sem, q_send, q_recv, part_send, part_recv, lse_send, lse_recv,
    heads_send, heads_recv, sums_send, sums_recv,
):
    n_ctx, n_seq, n_head = sizes
    ctx, seq, head = lax.axis_index("ctx"), lax.axis_index("seq"), lax.axis_index("head")
    rows, entries = q_raw.shape
    latent, places = own.shape[1], keys.shape[1]
    per_token = rows // DRAFT
    n_out = n_ctx * n_head
    place = ctx * n_head + head

    load_q = pltpu.make_async_copy(q_hbm, q_raw, load_sem.at[0])
    load_keys = pltpu.make_async_copy(keys_hbm, keys, load_sem.at[1])
    load_uv = pltpu.make_async_copy(w_uv_hbm, w_uv, load_sem.at[2])
    load_out = pltpu.make_async_copy(w_out_hbm, w_out, load_sem.at[3])
    load_q.start()
    load_keys.start()

    def row_device(k):
        other = lax.rem(place + k, n_out)
        return other, {"ctx": other // n_head, "head": lax.rem(other, n_head)}

    barrier = pltpu.get_barrier_semaphore()
    for k in range(1, n_out):
        pl.semaphore_signal(barrier, inc=1, device_id=row_device(k)[1], device_id_type=MESH)
    for k in range(1, n_seq):
        pl.semaphore_signal(
            barrier, inc=1, device_id={"seq": lax.rem(seq + k, n_seq)}, device_id_type=MESH
        )

    positions = [lengths[0] - DRAFT + offsets[0, t] for t in range(DRAFT)]
    limits = per_row(positions, (rows, 1), per_token)
    load_q.wait()
    latent_q = q_raw[:, :latent]
    rope_q = turned(q_raw[:, latent:].astype(jnp.float32), positions).astype(jnp.bfloat16)
    q_all[ctx, :, :latent] = latent_q
    q_all[ctx, :, latent:] = rope_q

    pl.semaphore_wait(barrier, n_out - 1 + n_seq - 1)

    toward = jnp.where(ctx < n_ctx // 2, 1, -1)
    shorter = jnp.minimum(ctx, n_ctx - 1 - ctx)

    def peer(k):
        near = jnp.where(lax.rem(k, 2) == 1, (k + 1) // 2, -(k // 2))
        return ctx + toward * jnp.where(k <= 2 * shorter, near, k - shorter)

    def q_copy(owner, side, send):
        return pltpu.make_async_remote_copy(
            src_ref=q_all.at[owner], dst_ref=q_all.at[owner],
            send_sem=q_send.at[send], recv_sem=q_recv.at[owner],
            device_id={"ctx": ctx + side}, device_id_type=MESH,
        )

    has_left, has_right = ctx > 0, ctx < n_ctx - 1

    @pl.when(has_right)
    def _():
        q_copy(ctx, 1, ctx).start()

    @pl.when(has_left)
    def _():
        q_copy(ctx, -1, n_ctx).start()

    def pass_on(distance):
        @pl.when(ctx - distance >= 0)
        def _():
            q_copy(ctx - distance, -1, 0).wait_recv()

            @pl.when(has_right)
            def _():
                q_copy(ctx - distance, 1, ctx - distance).start()

        @pl.when(ctx + distance < n_ctx)
        def _():
            q_copy(ctx + distance, 1, 0).wait_recv()

            @pl.when(has_left)
            def _():
                q_copy(ctx + distance, -1, ctx + distance).start()

    def part_copy(k, slot):
        return pltpu.make_async_remote_copy(
            src_ref=part_out.at[k], dst_ref=part_in.at[slot],
            send_sem=part_send.at[k], recv_sem=part_recv.at[slot],
            device_id={"ctx": peer(k)}, device_id_type=MESH,
        )

    def lse_copy(k, slot):
        return pltpu.make_async_remote_copy(
            src_ref=lse_out.at[k], dst_ref=lse_in.at[slot],
            send_sem=lse_send.at[k], recv_sem=lse_recv.at[slot],
            device_id={"ctx": peer(k)}, device_id_type=MESH,
        )

    load_keys.wait()
    load_uv.start()
    load_out.start()
    first_place = ctx * places

    narrow = next(c for c in (512, 256, LANES) if places % c == 0)
    wide = next(c for c in (1024, 512, 256, LANES) if places % c == 0)

    def folded(combine, total, chunk):
        for j in range(0, chunk.shape[1], LANES):
            total = combine(total, chunk[:, j : j + LANES])
        return total

    def attend(block):
        highest = jnp.full((rows, LANES), NEGATIVE, jnp.float32)
        for begin in range(0, places, narrow):
            some = slice(begin, begin + narrow)
            product = jnp.dot(block, keys[:, some], preferred_element_type=jnp.float32)
            place_of = lax.broadcasted_iota(jnp.int32, (1, narrow), 1)
            product = jnp.where(place_of <= limits - (first_place + begin), product, NEGATIVE)
            scores[:, some] = product
            highest = folded(jnp.maximum, highest, product)
        maxima = jnp.max(highest, axis=1, keepdims=True)
        sums_of = jnp.zeros((rows, LANES), jnp.float32)
        numerators = jnp.zeros((latent, rows), jnp.float32)
        for begin in range(0, places, wide):
            some = slice(begin, begin + wide)
            weights = jnp.exp2((scores[:, some] - maxima) * (SCALE / LN2))
            sums_of = folded(jnp.add, sums_of, weights)
            numerators = numerators + lax.dot_general(
                keys[:latent, some], weights.astype(jnp.bfloat16), (((1,), (1,)), ((), ())),
                preferred_element_type=jnp.float32,
            )
        totals = jnp.sum(sums_of, axis=1, keepdims=True)
        return numerators.T / totals, maxima * SCALE + jnp.log(totals)

    diagonal = lax.broadcasted_iota(jnp.int32, (rows, rows), 0) == lax.broadcasted_iota(
        jnp.int32, (rows, rows), 1
    )

    def send_part(k, part, lse):
        part_out[k] = part.astype(jnp.bfloat16)
        as_row = jnp.sum(jnp.where(diagonal, lse, 0.0), axis=0, keepdims=True)
        lse_out[k] = jnp.broadcast_to(as_row, lse_out.shape[1:])
        part_copy(k, ctx).start()
        lse_copy(k, ctx).start()

    def remote_block(k, carried):
        pass_on(k)
        send_part(k, *attend(q_all[peer(k)]))
        return carried

    own_part, own_lse = attend(q_all[ctx])
    own[...] = own_part
    lax.fori_loop(1, n_ctx, remote_block, 0)

    top = own_lse
    lses = []
    for k in range(1, n_ctx):
        slot = peer(k)
        lse_copy(k, slot).wait_recv()
        lse = jnp.sum(
            jnp.where(diagonal, lse_in[slot, 0:1, :], 0.0), axis=1, keepdims=True
        )
        lses.append(lse)
        top = jnp.maximum(top, lse)
    share = jnp.exp(own_lse - top)
    whole = share
    mixed = own[...] * share
    for k in range(1, n_ctx):
        slot = peer(k)
        part_copy(k, slot).wait_recv()
        share = jnp.exp(lses[k - 1] - top)
        whole = whole + share
        mixed = mixed + part_in[slot].astype(jnp.float32) * share
    mixed = mixed / whole
    for t in range(DRAFT):
        attended[t] = mixed[t * per_token : (t + 1) * per_token]

    load_uv.wait()
    vdim = w_uv.shape[2]
    for h in range(per_token):
        heads_all[seq, :, h * vdim : (h + 1) * vdim] = jnp.dot(
            attended[:, h, :].astype(jnp.bfloat16), w_uv[h], preferred_element_type=jnp.float32
        )

    def heads_copy(k, slot):
        return pltpu.make_async_remote_copy(
            src_ref=heads_all.at[seq], dst_ref=heads_all.at[slot],
            send_sem=heads_send.at[k], recv_sem=heads_recv.at[slot],
            device_id={"seq": lax.rem(seq + k, n_seq)}, device_id_type=MESH,
        )

    for k in range(1, n_seq):
        heads_copy(k, seq).start()
    columns = w_out.shape[1]
    n_parts = sums.shape[0]
    part_columns = columns // n_parts
    part_blocks = part_columns // LANES
    sums[...] = jnp.zeros_like(sums)
    load_out.wait()
    for k in range(1, n_seq):
        heads_copy(k, lax.rem(seq + k, n_seq)).wait_recv()
    tokens = jnp.concatenate([heads_all[s] for s in range(n_seq)], axis=0).astype(jnp.bfloat16)
    width = 2 * LANES if part_columns % (2 * LANES) == 0 else LANES

    def sums_copy(part, k, target, slot):
        return pltpu.make_async_remote_copy(
            src_ref=sums_out.at[part, target], dst_ref=sums_in.at[part, slot],
            send_sem=sums_send.at[part, k], recv_sem=sums_recv.at[part, slot],
            device_id=row_device(k)[1], device_id_type=MESH,
        )

    for part in range(n_parts):
        for first in range(0, part_columns, width):
            begin = part * part_columns + first
            product = jnp.dot(
                tokens, w_out[:, begin : begin + width], preferred_element_type=jnp.float32
            )
            for r in range(n_out):
                for i in range(width // LANES):
                    sums[part, r, first // LANES + i, :] = product[r, i * LANES : (i + 1) * LANES]
        for k in range(1, n_out):
            target = row_device(k)[0]
            sums_out[part, target] = sums[part, target].astype(jnp.bfloat16)
            sums_copy(part, k, target, place).start()
    for part in range(n_parts):
        result = sums[part, place]
        for k in range(1, n_out):
            slot = row_device(k)[0]
            sums_copy(part, k, slot, slot).wait_recv()
            result = result + sums_in[part, slot].astype(jnp.float32)
        for i in range(part_blocks):
            begin = part * part_columns + i * LANES
            out[:, begin : begin + LANES] = result[i : i + 1].astype(jnp.bfloat16)

    @pl.when(has_right)
    def _():
        q_copy(ctx, 1, ctx).wait_send()

    @pl.when(has_left)
    def _():
        q_copy(ctx, -1, n_ctx).wait_send()

    for k in range(1, n_ctx):
        @pl.when((ctx - k >= 0) & has_right)
        def _():
            q_copy(ctx - k, 1, ctx - k).wait_send()

        @pl.when((ctx + k < n_ctx) & has_left)
        def _():
            q_copy(ctx + k, -1, ctx + k).wait_send()

        part_copy(k, ctx).wait_send()
        lse_copy(k, ctx).wait_send()
    for k in range(1, n_seq):
        heads_copy(k, seq).wait_send()
    for part in range(n_parts):
        for k in range(1, n_out):
            sums_copy(part, k, row_device(k)[0], place).wait_send()


def per_device(sizes, queries, cache, lengths, offsets, w_uv, w_out):
    n_ctx, n_seq, n_head = sizes
    n_out = n_ctx * n_head
    heads, entries = queries.shape[2:]
    rows = DRAFT * heads
    places = cache.shape[1]
    latent, vdim = w_uv.shape[1:]
    columns = w_out.shape[1]
    n_blocks = columns // LANES
    n_parts = 2 if n_blocks % 2 == 0 else 1
    padded = -(-n_blocks // n_parts // 16) * 16
    sixteen, full = jnp.bfloat16, jnp.float32
    dma = pltpu.SemaphoreType.DMA
    smem = pl.BlockSpec(memory_space=pltpu.SMEM)
    anywhere = pl.BlockSpec(memory_space=pl.ANY)
    return pl.pallas_call(
        functools.partial(kernel, sizes),
        out_shape=jax.ShapeDtypeStruct((1, columns), sixteen),
        in_specs=[smem, smem, anywhere, anywhere, anywhere, anywhere],
        out_specs=pl.BlockSpec(memory_space=pltpu.VMEM),
        scratch_shapes=[
            pltpu.VMEM((rows, entries), sixteen),
            pltpu.VMEM((n_ctx, rows, entries), sixteen),
            pltpu.VMEM((entries, places), sixteen),
            pltpu.VMEM((rows, places), full),
            pltpu.VMEM(w_uv.shape, sixteen),
            pltpu.VMEM(w_out.shape, sixteen),
            pltpu.VMEM((rows, latent), full),
            pltpu.VMEM((n_ctx, rows, latent), sixteen),
            pltpu.VMEM((n_ctx, rows, latent), sixteen),
            pltpu.VMEM((n_ctx, 8, rows), full),
            pltpu.VMEM((n_ctx, 8, rows), full),
            pltpu.VMEM((DRAFT, heads, latent), full),
            pltpu.VMEM((n_seq, DRAFT, heads * vdim), full),
            pltpu.VMEM((n_parts, n_out, padded, LANES), full),
            pltpu.VMEM((n_parts, n_out, padded, LANES), sixteen),
            pltpu.VMEM((n_parts, n_out, padded, LANES), sixteen),
            dma((4,)),
            dma((n_ctx + 1,)), dma((n_ctx,)),
            dma((n_ctx,)), dma((n_ctx,)),
            dma((n_ctx,)), dma((n_ctx,)),
            dma((n_seq,)), dma((n_seq,)),
            dma((n_parts, n_out)), dma((n_parts, n_out)),
        ],
        compiler_params=pltpu.CompilerParams(
            collective_id=0, has_side_effects=True, vmem_limit_bytes=60 * 2**20
        ),
        name="latent_attention",
    )(
        lengths,
        offsets,
        queries.reshape(rows, entries),
        jnp.swapaxes(cache[0], 0, 1),
        w_uv,
        w_out,
    )


def solution(mesh):
    sizes = (mesh.shape["ctx"], mesh.shape["seq"], mesh.shape["head"])
    in_specs = (
        P(("groups", "seq"), None, ("ctx", "head"), None),
        P(("groups", "seq"), "ctx", None),
        P(("groups", "seq")),
        P(("groups", "seq"), None),
        P(("ctx", "head"), None, None),
        P(("ctx", "head"), "seq"),
    )
    out_specs = P(("groups", "ctx", "head"), "seq")
    return jax.shard_map(
        functools.partial(per_device, sizes),
        mesh=mesh, in_specs=in_specs, out_specs=out_specs, check_vma=False,
    )
```

```python
import functools
import math

import jax
import jax.numpy as jnp
from jax import lax
from jax.experimental import pallas as pl
from jax.experimental.pallas import tpu as pltpu
from jax.sharding import PartitionSpec as P

ROPE = 64
NOPE = 128
DRAFT = 4
LANES = 128
THETA = 10000.0
NEGATIVE = -1e30
SCALE = (NOPE + ROPE) ** -0.5
LN2 = math.log(2.0)
TURN = 2.0 * math.pi
TURN_HIGH = 6.28125
TURN_MID = math.floor((TURN - TURN_HIGH) * 2**19) / 2**19
TURN_LOW = TURN - TURN_HIGH - TURN_MID
MESH = pl.DeviceIdType.MESH


def sine_cosine(angle):
    turns = jnp.floor(angle * (1.0 / TURN) + 0.5)
    r = ((angle - turns * TURN_HIGH) - turns * TURN_MID) - turns * TURN_LOW
    square = r * r
    sine = jnp.zeros_like(r)
    cosine = jnp.zeros_like(r)
    for i in range(9, -1, -1):
        sign = -1.0 if i % 2 else 1.0
        cosine = cosine * square + sign / math.factorial(2 * i)
        sine = sine * square + sign / math.factorial(2 * i + 1)
    return sine * r, cosine


def per_row(scalars, shape, per_token):
    row = lax.broadcasted_iota(jnp.int32, shape, 0)
    column = jnp.full(shape, scalars[-1])
    for t in range(len(scalars) - 2, -1, -1):
        column = jnp.where(row < (t + 1) * per_token, scalars[t], column)
    return column


def turned(rope, positions):
    rows = rope.shape[0]
    half = ROPE // 2
    lane = lax.broadcasted_iota(jnp.int32, (1, ROPE), 1)
    frequency = jnp.zeros((1, ROPE), jnp.float32)
    for i in range(half):
        frequency = jnp.where(lane % half == i, THETA ** (-2.0 * i / ROPE), frequency)
    position = per_row(positions, (rows, ROPE), rows // DRAFT).astype(jnp.float32)
    sine, cosine = sine_cosine(position * frequency)
    swapped = jnp.concatenate([rope[:, half:], rope[:, :half]], axis=1)
    return rope * cosine + jnp.where(lane < half, -swapped, swapped) * sine


def kernel(
    sizes,
    lengths, offsets, q_hbm, keys_hbm, w_uv_hbm, w_out_hbm,
    out,
    q_raw, q_all, keys, scores, w_uv, w_out, own, part_out, part_in, lse_out, lse_in,
    attended, heads_all, sums, sums_out, sums_in,
    load_sem, out_sem, q_send, q_recv, part_send, part_recv, lse_send, lse_recv,
    heads_send, heads_recv, sums_send, sums_recv,
):
    n_ctx, n_seq, n_head = sizes
    ctx, seq, head = lax.axis_index("ctx"), lax.axis_index("seq"), lax.axis_index("head")
    rows, entries = q_raw.shape
    latent, places = own.shape[1], keys.shape[1]
    per_token = rows // DRAFT
    n_out = n_ctx * n_head
    place = ctx * n_head + head

    load_q = pltpu.make_async_copy(q_hbm, q_raw, load_sem.at[0])
    load_keys = pltpu.make_async_copy(keys_hbm, keys, load_sem.at[1])
    load_uv = pltpu.make_async_copy(w_uv_hbm, w_uv, load_sem.at[2])
    pieces = out_sem.shape[0]
    piece_rows = w_out.shape[0] // pieces

    def load_out(i):
        piece = pl.ds(pl.multiple_of(i * piece_rows, piece_rows), piece_rows)
        return pltpu.make_async_copy(w_out_hbm.at[piece], w_out.at[piece], out_sem.at[i])

    load_q.start()
    load_keys.start()

    def row_device(k):
        other = lax.rem(place + k, n_out)
        return other, {"ctx": other // n_head, "head": lax.rem(other, n_head)}

    barrier = pltpu.get_barrier_semaphore()
    for k in range(1, n_out):
        pl.semaphore_signal(barrier, inc=1, device_id=row_device(k)[1], device_id_type=MESH)
    for k in range(1, n_seq):
        pl.semaphore_signal(
            barrier, inc=1, device_id={"seq": lax.rem(seq + k, n_seq)}, device_id_type=MESH
        )

    positions = [lengths[0] - DRAFT + offsets[0, t] for t in range(DRAFT)]
    limits = per_row(positions, (rows, 1), per_token)
    load_q.wait()
    latent_q = q_raw[:, :latent]
    rope_q = turned(q_raw[:, latent:].astype(jnp.float32), positions).astype(jnp.bfloat16)
    q_all[ctx, :, :latent] = latent_q
    q_all[ctx, :, latent:] = rope_q

    pl.semaphore_wait(barrier, n_out - 1 + n_seq - 1)

    toward = jnp.where(ctx < n_ctx // 2, 1, -1)
    shorter = jnp.minimum(ctx, n_ctx - 1 - ctx)

    def peer(k):
        near = jnp.where(lax.rem(k, 2) == 1, (k + 1) // 2, -(k // 2))
        return ctx + toward * jnp.where(k <= 2 * shorter, near, k - shorter)

    def q_copy(owner, side, send):
        return pltpu.make_async_remote_copy(
            src_ref=q_all.at[owner], dst_ref=q_all.at[owner],
            send_sem=q_send.at[send], recv_sem=q_recv.at[owner],
            device_id={"ctx": ctx + side}, device_id_type=MESH,
        )

    has_left, has_right = ctx > 0, ctx < n_ctx - 1

    @pl.when(has_right)
    def _():
        q_copy(ctx, 1, ctx).start()

    @pl.when(has_left)
    def _():
        q_copy(ctx, -1, n_ctx).start()

    def pass_on(distance):
        @pl.when(ctx - distance >= 0)
        def _():
            q_copy(ctx - distance, -1, 0).wait_recv()

            @pl.when(has_right)
            def _():
                q_copy(ctx - distance, 1, ctx - distance).start()

        @pl.when(ctx + distance < n_ctx)
        def _():
            q_copy(ctx + distance, 1, 0).wait_recv()

            @pl.when(has_left)
            def _():
                q_copy(ctx + distance, -1, ctx + distance).start()

    def part_copy(k, slot):
        return pltpu.make_async_remote_copy(
            src_ref=part_out.at[k], dst_ref=part_in.at[slot],
            send_sem=part_send.at[k], recv_sem=part_recv.at[slot],
            device_id={"ctx": peer(k)}, device_id_type=MESH,
        )

    def lse_copy(k, slot):
        return pltpu.make_async_remote_copy(
            src_ref=lse_out.at[k], dst_ref=lse_in.at[slot],
            send_sem=lse_send.at[k], recv_sem=lse_recv.at[slot],
            device_id={"ctx": peer(k)}, device_id_type=MESH,
        )

    load_keys.wait()
    for i in range(pieces // n_ctx):
        load_out(i).start()
    first_place = ctx * places

    narrow = next(c for c in (512, 256, LANES) if places % c == 0)
    wide = next(c for c in (1024, 512, 256, LANES) if places % c == 0)

    def folded(combine, total, chunk):
        for j in range(0, chunk.shape[1], LANES):
            total = combine(total, chunk[:, j : j + LANES])
        return total

    def attend(block):
        highest = jnp.full((rows, LANES), NEGATIVE, jnp.float32)
        for begin in range(0, places, narrow):
            some = slice(begin, begin + narrow)
            product = jnp.dot(block, keys[:, some], preferred_element_type=jnp.float32)
            place_of = lax.broadcasted_iota(jnp.int32, (1, narrow), 1)
            product = jnp.where(place_of <= limits - (first_place + begin), product, NEGATIVE)
            scores[:, some] = product
            highest = folded(jnp.maximum, highest, product)
        maxima = jnp.max(highest, axis=1, keepdims=True)
        sums_of = jnp.zeros((rows, LANES), jnp.float32)
        numerators = jnp.zeros((latent, rows), jnp.float32)
        for begin in range(0, places, wide):
            some = slice(begin, begin + wide)
            weights = jnp.exp2((scores[:, some] - maxima) * (SCALE / LN2))
            sums_of = folded(jnp.add, sums_of, weights)
            numerators = numerators + lax.dot_general(
                keys[:latent, some], weights.astype(jnp.bfloat16), (((1,), (1,)), ((), ())),
                preferred_element_type=jnp.float32,
            )
        totals = jnp.sum(sums_of, axis=1, keepdims=True)
        return numerators.T * (1.0 / totals), maxima * SCALE + jnp.log(totals)

    diagonal = lax.broadcasted_iota(jnp.int32, (rows, rows), 0) == lax.broadcasted_iota(
        jnp.int32, (rows, rows), 1
    )

    def send_part(k, part, lse):
        part_out[k] = part.astype(jnp.bfloat16)
        as_row = jnp.sum(jnp.where(diagonal, lse, 0.0), axis=0, keepdims=True)
        lse_out[k] = jnp.broadcast_to(as_row, lse_out.shape[1:])
        part_copy(k, ctx).start()
        lse_copy(k, ctx).start()

    def remote_block(k, carried):
        pass_on(k)
        for i in range(pieces // n_ctx):
            load_out(k * (pieces // n_ctx) + i).start()

        @pl.when(k == n_ctx - 1)
        def _():
            load_uv.start()

        send_part(k, *attend(q_all[peer(k)]))
        return carried

    own_part, own_lse = attend(q_all[ctx])
    own[...] = own_part
    lax.fori_loop(1, n_ctx, remote_block, 0)

    top = own_lse
    lses = []
    for k in range(1, n_ctx):
        slot = peer(k)
        lse_copy(k, slot).wait_recv()
        lse = jnp.sum(
            jnp.where(diagonal, lse_in[slot, 0:1, :], 0.0), axis=1, keepdims=True
        )
        lses.append(lse)
        top = jnp.maximum(top, lse)
    share = jnp.exp(own_lse - top)
    whole = share
    mixed = own[...] * share
    for k in range(1, n_ctx):
        slot = peer(k)
        part_copy(k, slot).wait_recv()
        share = jnp.exp(lses[k - 1] - top)
        whole = whole + share
        mixed = mixed + part_in[slot].astype(jnp.float32) * share
    mixed = mixed / whole
    for t in range(DRAFT):
        attended[t] = mixed[t * per_token : (t + 1) * per_token]

    load_uv.wait()
    vdim = w_uv.shape[2]
    for h in range(per_token):
        heads_all[seq, :, h * vdim : (h + 1) * vdim] = jnp.dot(
            attended[:, h, :].astype(jnp.bfloat16), w_uv[h], preferred_element_type=jnp.float32
        )

    def heads_copy(k, slot):
        return pltpu.make_async_remote_copy(
            src_ref=heads_all.at[seq], dst_ref=heads_all.at[slot],
            send_sem=heads_send.at[k], recv_sem=heads_recv.at[slot],
            device_id={"seq": lax.rem(seq + k, n_seq)}, device_id_type=MESH,
        )

    for k in range(1, n_seq):
        heads_copy(k, seq).start()
    columns = w_out.shape[1]
    n_parts = sums.shape[0]
    part_columns = columns // n_parts
    part_blocks = part_columns // LANES
    sums[...] = jnp.zeros_like(sums)
    for i in range(pieces):
        load_out(i).wait()
    for k in range(1, n_seq):
        heads_copy(k, lax.rem(seq + k, n_seq)).wait_recv()
    tokens = jnp.concatenate([heads_all[s] for s in range(n_seq)], axis=0).astype(jnp.bfloat16)
    width = 2 * LANES if part_columns % (2 * LANES) == 0 else LANES

    def sums_copy(part, k, target, slot):
        return pltpu.make_async_remote_copy(
            src_ref=sums_out.at[part, target], dst_ref=sums_in.at[part, slot],
            send_sem=sums_send.at[part, k], recv_sem=sums_recv.at[part, slot],
            device_id=row_device(k)[1], device_id_type=MESH,
        )

    for part in range(n_parts):
        for first in range(0, part_columns, width):
            begin = part * part_columns + first
            product = jnp.dot(
                tokens, w_out[:, begin : begin + width], preferred_element_type=jnp.float32
            )
            for r in range(n_out):
                for i in range(width // LANES):
                    sums[part, r, first // LANES + i, :] = product[r, i * LANES : (i + 1) * LANES]
        for k in range(1, n_out):
            target = row_device(k)[0]
            sums_out[part, target] = sums[part, target].astype(jnp.bfloat16)
            sums_copy(part, k, target, place).start()
    for part in range(n_parts):
        result = sums[part, place]
        for k in range(1, n_out):
            slot = row_device(k)[0]
            sums_copy(part, k, slot, slot).wait_recv()
            result = result + sums_in[part, slot].astype(jnp.float32)
        for i in range(part_blocks):
            begin = part * part_columns + i * LANES
            out[:, begin : begin + LANES] = result[i : i + 1].astype(jnp.bfloat16)

    @pl.when(has_right)
    def _():
        q_copy(ctx, 1, ctx).wait_send()

    @pl.when(has_left)
    def _():
        q_copy(ctx, -1, n_ctx).wait_send()

    for k in range(1, n_ctx):
        @pl.when((ctx - k >= 0) & has_right)
        def _():
            q_copy(ctx - k, 1, ctx - k).wait_send()

        @pl.when((ctx + k < n_ctx) & has_left)
        def _():
            q_copy(ctx + k, -1, ctx + k).wait_send()

        part_copy(k, ctx).wait_send()
        lse_copy(k, ctx).wait_send()
    for k in range(1, n_seq):
        heads_copy(k, seq).wait_send()
    for part in range(n_parts):
        for k in range(1, n_out):
            sums_copy(part, k, row_device(k)[0], place).wait_send()


def per_device(sizes, queries, cache, lengths, offsets, w_uv, w_out):
    n_ctx, n_seq, n_head = sizes
    n_out = n_ctx * n_head
    heads, entries = queries.shape[2:]
    rows = DRAFT * heads
    places = cache.shape[1]
    latent, vdim = w_uv.shape[1:]
    columns = w_out.shape[1]
    n_blocks = columns // LANES
    n_parts = 2 if n_blocks % 2 == 0 else 1
    padded = -(-n_blocks // n_parts // 16) * 16
    sixteen, full = jnp.bfloat16, jnp.float32
    dma = pltpu.SemaphoreType.DMA
    smem = pl.BlockSpec(memory_space=pltpu.SMEM)
    anywhere = pl.BlockSpec(memory_space=pl.ANY)
    return pl.pallas_call(
        functools.partial(kernel, sizes),
        out_shape=jax.ShapeDtypeStruct((1, columns), sixteen),
        in_specs=[smem, smem, anywhere, anywhere, anywhere, anywhere],
        out_specs=pl.BlockSpec(memory_space=pltpu.VMEM),
        scratch_shapes=[
            pltpu.VMEM((rows, entries), sixteen),
            pltpu.VMEM((n_ctx, rows, entries), sixteen),
            pltpu.VMEM((entries, places), sixteen),
            pltpu.VMEM((rows, places), full),
            pltpu.VMEM(w_uv.shape, sixteen),
            pltpu.VMEM(w_out.shape, sixteen),
            pltpu.VMEM((rows, latent), full),
            pltpu.VMEM((n_ctx, rows, latent), sixteen),
            pltpu.VMEM((n_ctx, rows, latent), sixteen),
            pltpu.VMEM((n_ctx, 8, rows), full),
            pltpu.VMEM((n_ctx, 8, rows), full),
            pltpu.VMEM((DRAFT, heads, latent), full),
            pltpu.VMEM((n_seq, DRAFT, heads * vdim), full),
            pltpu.VMEM((n_parts, n_out, padded, LANES), full),
            pltpu.VMEM((n_parts, n_out, padded, LANES), sixteen),
            pltpu.VMEM((n_parts, n_out, padded, LANES), sixteen),
            dma((3,)), dma((n_ctx * max(1, 16 // n_ctx),)),
            dma((n_ctx + 1,)), dma((n_ctx,)),
            dma((n_ctx,)), dma((n_ctx,)),
            dma((n_ctx,)), dma((n_ctx,)),
            dma((n_seq,)), dma((n_seq,)),
            dma((n_parts, n_out)), dma((n_parts, n_out)),
        ],
        compiler_params=pltpu.CompilerParams(
            collective_id=0, has_side_effects=True, vmem_limit_bytes=60 * 2**20
        ),
        name="latent_attention",
    )(
        lengths,
        offsets,
        queries.reshape(rows, entries),
        jnp.swapaxes(cache[0], 0, 1),
        w_uv,
        w_out,
    )


def solution(mesh):
    sizes = (mesh.shape["ctx"], mesh.shape["seq"], mesh.shape["head"])
    in_specs = (
        P(("groups", "seq"), None, ("ctx", "head"), None),
        P(("groups", "seq"), "ctx", None),
        P(("groups", "seq")),
        P(("groups", "seq"), None),
        P(("ctx", "head"), None, None),
        P(("ctx", "head"), "seq"),
    )
    out_specs = P(("groups", "ctx", "head"), "seq")
    return jax.shard_map(
        functools.partial(per_device, sizes),
        mesh=mesh, in_specs=in_specs, out_specs=out_specs, check_vma=False,
    )
```

```python
import functools
import math

import jax
import jax.numpy as jnp
from jax import lax
from jax.experimental import pallas as pl
from jax.experimental.pallas import tpu as pltpu
from jax.sharding import PartitionSpec as P

ROPE = 64
NOPE = 128
DRAFT = 4
LANES = 128
THETA = 10000.0
NEGATIVE = -1e30
SCALE = (NOPE + ROPE) ** -0.5
LN2 = math.log(2.0)
TURN = 2.0 * math.pi
TURN_HIGH = 6.28125
TURN_MID = math.floor((TURN - TURN_HIGH) * 2**19) / 2**19
TURN_LOW = TURN - TURN_HIGH - TURN_MID
MESH = pl.DeviceIdType.MESH


def sine_cosine(angle):
    turns = jnp.floor(angle * (1.0 / TURN) + 0.5)
    r = ((angle - turns * TURN_HIGH) - turns * TURN_MID) - turns * TURN_LOW
    square = r * r
    sine = jnp.zeros_like(r)
    cosine = jnp.zeros_like(r)
    for i in range(9, -1, -1):
        sign = -1.0 if i % 2 else 1.0
        cosine = cosine * square + sign / math.factorial(2 * i)
        sine = sine * square + sign / math.factorial(2 * i + 1)
    return sine * r, cosine


def per_row(scalars, shape, per_token):
    row = lax.broadcasted_iota(jnp.int32, shape, 0)
    column = jnp.full(shape, scalars[-1])
    for t in range(len(scalars) - 2, -1, -1):
        column = jnp.where(row < (t + 1) * per_token, scalars[t], column)
    return column


def turned(rope, positions):
    rows = rope.shape[0]
    half = ROPE // 2
    lane = lax.broadcasted_iota(jnp.int32, (1, ROPE), 1)
    frequency = jnp.zeros((1, ROPE), jnp.float32)
    for i in range(half):
        frequency = jnp.where(lane % half == i, THETA ** (-2.0 * i / ROPE), frequency)
    position = per_row(positions, (rows, ROPE), rows // DRAFT).astype(jnp.float32)
    sine, cosine = sine_cosine(position * frequency)
    swapped = jnp.concatenate([rope[:, half:], rope[:, :half]], axis=1)
    return rope * cosine + jnp.where(lane < half, -swapped, swapped) * sine


def kernel(
    sizes,
    lengths, offsets, q_hbm, keys_hbm, w_uv_hbm, w_out_hbm,
    out,
    q_raw, q_all, keys, values, w_uv, w_out, own, part_out, part_in, lse_out, lse_in,
    attended, heads_all, sums, sums_out, sums_in,
    load_sem, q_send, q_recv, part_send, part_recv, lse_send, lse_recv,
    heads_send, heads_recv, sums_send, sums_recv,
):
    n_ctx, n_seq, n_head = sizes
    ctx, seq, head = lax.axis_index("ctx"), lax.axis_index("seq"), lax.axis_index("head")
    rows, entries = q_raw.shape
    latent, places = own.shape[1], keys.shape[1]
    per_token = rows // DRAFT
    n_out = n_ctx * n_head
    place = ctx * n_head + head

    load_q = pltpu.make_async_copy(q_hbm, q_raw, load_sem.at[0])
    load_keys = pltpu.make_async_copy(keys_hbm, keys, load_sem.at[1])
    load_uv = pltpu.make_async_copy(w_uv_hbm, w_uv, load_sem.at[2])
    load_out = pltpu.make_async_copy(w_out_hbm, w_out, load_sem.at[3])
    load_q.start()
    load_keys.start()

    def row_device(k):
        other = lax.rem(place + k, n_out)
        return other, {"ctx": other // n_head, "head": lax.rem(other, n_head)}

    barrier = pltpu.get_barrier_semaphore()
    for k in range(1, n_out):
        pl.semaphore_signal(barrier, inc=1, device_id=row_device(k)[1], device_id_type=MESH)
    for k in range(1, n_seq):
        pl.semaphore_signal(
            barrier, inc=1, device_id={"seq": lax.rem(seq + k, n_seq)}, device_id_type=MESH
        )

    positions = [lengths[0] - DRAFT + offsets[0, t] for t in range(DRAFT)]
    limits = per_row(positions, (rows, 1), per_token)
    load_q.wait()
    latent_q = q_raw[:, :latent]
    rope_q = turned(q_raw[:, latent:].astype(jnp.float32), positions).astype(jnp.bfloat16)
    q_all[ctx, :, :latent] = latent_q
    q_all[ctx, :, latent:] = rope_q

    pl.semaphore_wait(barrier, n_out - 1 + n_seq - 1)

    toward = jnp.where(ctx < n_ctx // 2, 1, -1)
    shorter = jnp.minimum(ctx, n_ctx - 1 - ctx)

    def peer(k):
        near = jnp.where(lax.rem(k, 2) == 1, (k + 1) // 2, -(k // 2))
        return ctx + toward * jnp.where(k <= 2 * shorter, near, k - shorter)

    def q_copy(owner, side, send):
        return pltpu.make_async_remote_copy(
            src_ref=q_all.at[owner], dst_ref=q_all.at[owner],
            send_sem=q_send.at[send], recv_sem=q_recv.at[owner],
            device_id={"ctx": ctx + side}, device_id_type=MESH,
        )

    has_left, has_right = ctx > 0, ctx < n_ctx - 1

    @pl.when(has_right)
    def _():
        q_copy(ctx, 1, ctx).start()

    @pl.when(has_left)
    def _():
        q_copy(ctx, -1, n_ctx).start()

    def pass_on(distance):
        @pl.when(ctx - distance >= 0)
        def _():
            q_copy(ctx - distance, -1, 0).wait_recv()

            @pl.when(has_right)
            def _():
                q_copy(ctx - distance, 1, ctx - distance).start()

        @pl.when(ctx + distance < n_ctx)
        def _():
            q_copy(ctx + distance, 1, 0).wait_recv()

            @pl.when(has_left)
            def _():
                q_copy(ctx + distance, -1, ctx + distance).start()

    def part_copy(k, slot):
        return pltpu.make_async_remote_copy(
            src_ref=part_out.at[k], dst_ref=part_in.at[slot],
            send_sem=part_send.at[k], recv_sem=part_recv.at[slot],
            device_id={"ctx": peer(k)}, device_id_type=MESH,
        )

    def lse_copy(k, slot):
        return pltpu.make_async_remote_copy(
            src_ref=lse_out.at[k], dst_ref=lse_in.at[slot],
            send_sem=lse_send.at[k], recv_sem=lse_recv.at[slot],
            device_id={"ctx": peer(k)}, device_id_type=MESH,
        )

    load_keys.wait()
    load_uv.start()
    load_out.start()
    first_place = ctx * places

    def weigh(block):
        scores = jnp.dot(block, keys[...], preferred_element_type=jnp.float32)
        place_of = lax.broadcasted_iota(jnp.int32, (1, places), 1)
        scores = jnp.where(place_of <= limits - first_place, scores, NEGATIVE)
        maxima = jnp.max(scores, axis=1, keepdims=True)
        weights = jnp.exp2((scores - maxima) * (SCALE / LN2))
        totals = jnp.sum(weights, axis=1, keepdims=True)
        return weights.astype(jnp.bfloat16), 1.0 / totals, maxima * SCALE + jnp.log(totals)

    def attend_own(block):
        weights, inverse, lse = weigh(block)
        tile = next(c for c in (256, LANES) if places % c == 0)
        row = lax.broadcasted_iota(jnp.int32, (tile, tile), 0)
        column = lax.broadcasted_iota(jnp.int32, (tile, tile), 1)
        identity = (row == column).astype(jnp.float32).astype(jnp.bfloat16)
        numerators = jnp.zeros((rows, latent), jnp.float32)
        for begin in range(0, places, tile):
            some = slice(begin, begin + tile)
            product = lax.dot_general(
                jnp.concatenate([identity, weights[:, some]], axis=0), keys[:latent, some],
                (((1,), (1,)), ((), ())), preferred_element_type=jnp.float32,
            )
            values[some, :] = product[:tile].astype(jnp.bfloat16)
            numerators = numerators + product[tile:]
        return numerators * inverse, lse

    def attend(block):
        weights, inverse, lse = weigh(block)
        return jnp.dot(weights, values[...], preferred_element_type=jnp.float32) * inverse, lse

    diagonal = lax.broadcasted_iota(jnp.int32, (rows, rows), 0) == lax.broadcasted_iota(
        jnp.int32, (rows, rows), 1
    )

    def send_part(k, part, lse):
        part_out[k] = part.astype(jnp.bfloat16)
        as_row = jnp.sum(jnp.where(diagonal, lse, 0.0), axis=0, keepdims=True)
        lse_out[k] = jnp.broadcast_to(as_row, lse_out.shape[1:])
        part_copy(k, ctx).start()
        lse_copy(k, ctx).start()

    def remote_block(k, carried):
        pass_on(k)
        send_part(k, *attend(q_all[peer(k)]))
        return carried

    own_part, own_lse = attend_own(q_all[ctx])
    own[...] = own_part
    lax.fori_loop(1, n_ctx, remote_block, 0)

    top = own_lse
    lses = []
    for k in range(1, n_ctx):
        slot = peer(k)
        lse_copy(k, slot).wait_recv()
        lse = jnp.sum(
            jnp.where(diagonal, lse_in[slot, 0:1, :], 0.0), axis=1, keepdims=True
        )
        lses.append(lse)
        top = jnp.maximum(top, lse)
    share = jnp.exp(own_lse - top)
    whole = share
    mixed = own[...] * share
    for k in range(1, n_ctx):
        slot = peer(k)
        part_copy(k, slot).wait_recv()
        share = jnp.exp(lses[k - 1] - top)
        whole = whole + share
        mixed = mixed + part_in[slot].astype(jnp.float32) * share
    mixed = mixed / whole
    for t in range(DRAFT):
        attended[t] = mixed[t * per_token : (t + 1) * per_token]

    load_uv.wait()
    vdim = w_uv.shape[2]
    for h in range(per_token):
        heads_all[seq, :, h * vdim : (h + 1) * vdim] = jnp.dot(
            attended[:, h, :].astype(jnp.bfloat16), w_uv[h], preferred_element_type=jnp.float32
        )

    def heads_copy(k, slot):
        return pltpu.make_async_remote_copy(
            src_ref=heads_all.at[seq], dst_ref=heads_all.at[slot],
            send_sem=heads_send.at[k], recv_sem=heads_recv.at[slot],
            device_id={"seq": lax.rem(seq + k, n_seq)}, device_id_type=MESH,
        )

    for k in range(1, n_seq):
        heads_copy(k, seq).start()
    columns = w_out.shape[1]
    n_parts = sums.shape[0]
    part_columns = columns // n_parts
    part_blocks = part_columns // LANES
    sums[...] = jnp.zeros_like(sums)
    load_out.wait()
    for k in range(1, n_seq):
        heads_copy(k, lax.rem(seq + k, n_seq)).wait_recv()
    tokens = jnp.concatenate([heads_all[s] for s in range(n_seq)], axis=0).astype(jnp.bfloat16)
    width = 2 * LANES if part_columns % (2 * LANES) == 0 else LANES

    def sums_copy(part, k, target, slot):
        return pltpu.make_async_remote_copy(
            src_ref=sums_out.at[part, target], dst_ref=sums_in.at[part, slot],
            send_sem=sums_send.at[part, k], recv_sem=sums_recv.at[part, slot],
            device_id=row_device(k)[1], device_id_type=MESH,
        )

    for part in range(n_parts):
        for first in range(0, part_columns, width):
            begin = part * part_columns + first
            product = jnp.dot(
                tokens, w_out[:, begin : begin + width], preferred_element_type=jnp.float32
            )
            for r in range(n_out):
                for i in range(width // LANES):
                    sums[part, r, first // LANES + i, :] = product[r, i * LANES : (i + 1) * LANES]
        for k in range(1, n_out):
            target = row_device(k)[0]
            sums_out[part, target] = sums[part, target].astype(jnp.bfloat16)
            sums_copy(part, k, target, place).start()
    for part in range(n_parts):
        result = sums[part, place]
        for k in range(1, n_out):
            slot = row_device(k)[0]
            sums_copy(part, k, slot, slot).wait_recv()
            result = result + sums_in[part, slot].astype(jnp.float32)
        for i in range(part_blocks):
            begin = part * part_columns + i * LANES
            out[:, begin : begin + LANES] = result[i : i + 1].astype(jnp.bfloat16)

    @pl.when(has_right)
    def _():
        q_copy(ctx, 1, ctx).wait_send()

    @pl.when(has_left)
    def _():
        q_copy(ctx, -1, n_ctx).wait_send()

    for k in range(1, n_ctx):
        @pl.when((ctx - k >= 0) & has_right)
        def _():
            q_copy(ctx - k, 1, ctx - k).wait_send()

        @pl.when((ctx + k < n_ctx) & has_left)
        def _():
            q_copy(ctx + k, -1, ctx + k).wait_send()

        part_copy(k, ctx).wait_send()
        lse_copy(k, ctx).wait_send()
    for k in range(1, n_seq):
        heads_copy(k, seq).wait_send()
    for part in range(n_parts):
        for k in range(1, n_out):
            sums_copy(part, k, row_device(k)[0], place).wait_send()


def per_device(sizes, queries, cache, lengths, offsets, w_uv, w_out):
    n_ctx, n_seq, n_head = sizes
    n_out = n_ctx * n_head
    heads, entries = queries.shape[2:]
    rows = DRAFT * heads
    places = cache.shape[1]
    latent, vdim = w_uv.shape[1:]
    columns = w_out.shape[1]
    n_blocks = columns // LANES
    n_parts = 2 if n_blocks % 2 == 0 else 1
    padded = -(-n_blocks // n_parts // 16) * 16
    sixteen, full = jnp.bfloat16, jnp.float32
    dma = pltpu.SemaphoreType.DMA
    smem = pl.BlockSpec(memory_space=pltpu.SMEM)
    anywhere = pl.BlockSpec(memory_space=pl.ANY)
    return pl.pallas_call(
        functools.partial(kernel, sizes),
        out_shape=jax.ShapeDtypeStruct((1, columns), sixteen),
        in_specs=[smem, smem, anywhere, anywhere, anywhere, anywhere],
        out_specs=pl.BlockSpec(memory_space=pltpu.VMEM),
        scratch_shapes=[
            pltpu.VMEM((rows, entries), sixteen),
            pltpu.VMEM((n_ctx, rows, entries), sixteen),
            pltpu.VMEM((entries, places), sixteen),
            pltpu.VMEM((places, latent), sixteen),
            pltpu.VMEM(w_uv.shape, sixteen),
            pltpu.VMEM(w_out.shape, sixteen),
            pltpu.VMEM((rows, latent), full),
            pltpu.VMEM((n_ctx, rows, latent), sixteen),
            pltpu.VMEM((n_ctx, rows, latent), sixteen),
            pltpu.VMEM((n_ctx, 8, rows), full),
            pltpu.VMEM((n_ctx, 8, rows), full),
            pltpu.VMEM((DRAFT, heads, latent), full),
            pltpu.VMEM((n_seq, DRAFT, heads * vdim), full),
            pltpu.VMEM((n_parts, n_out, padded, LANES), full),
            pltpu.VMEM((n_parts, n_out, padded, LANES), sixteen),
            pltpu.VMEM((n_parts, n_out, padded, LANES), sixteen),
            dma((4,)),
            dma((n_ctx + 1,)), dma((n_ctx,)),
            dma((n_ctx,)), dma((n_ctx,)),
            dma((n_ctx,)), dma((n_ctx,)),
            dma((n_seq,)), dma((n_seq,)),
            dma((n_parts, n_out)), dma((n_parts, n_out)),
        ],
        compiler_params=pltpu.CompilerParams(
            collective_id=0, has_side_effects=True, vmem_limit_bytes=60 * 2**20
        ),
        name="latent_attention",
    )(
        lengths,
        offsets,
        queries.reshape(rows, entries),
        jnp.swapaxes(cache[0], 0, 1),
        w_uv,
        w_out,
    )


def solution(mesh):
    sizes = (mesh.shape["ctx"], mesh.shape["seq"], mesh.shape["head"])
    in_specs = (
        P(("groups", "seq"), None, ("ctx", "head"), None),
        P(("groups", "seq"), "ctx", None),
        P(("groups", "seq")),
        P(("groups", "seq"), None),
        P(("ctx", "head"), None, None),
        P(("ctx", "head"), "seq"),
    )
    out_specs = P(("groups", "ctx", "head"), "seq")
    return jax.shard_map(
        functools.partial(per_device, sizes),
        mesh=mesh, in_specs=in_specs, out_specs=out_specs, check_vma=False,
    )
```

```python
import functools
import math

import jax
import jax.numpy as jnp
from jax import lax
from jax.experimental import pallas as pl
from jax.experimental.pallas import tpu as pltpu
from jax.sharding import PartitionSpec as P

ROPE = 64
NOPE = 128
DRAFT = 4
LANES = 128
THETA = 10000.0
NEGATIVE = -1e30
SCALE = (NOPE + ROPE) ** -0.5
LN2 = math.log(2.0)
TURN = 2.0 * math.pi
TURN_HIGH = 6.28125
TURN_MID = math.floor((TURN - TURN_HIGH) * 2**19) / 2**19
TURN_LOW = TURN - TURN_HIGH - TURN_MID
MESH = pl.DeviceIdType.MESH


def sine_cosine(angle):
    turns = jnp.floor(angle * (1.0 / TURN) + 0.5)
    r = ((angle - turns * TURN_HIGH) - turns * TURN_MID) - turns * TURN_LOW
    square = r * r
    sine = jnp.zeros_like(r)
    cosine = jnp.zeros_like(r)
    for i in range(9, -1, -1):
        sign = -1.0 if i % 2 else 1.0
        cosine = cosine * square + sign / math.factorial(2 * i)
        sine = sine * square + sign / math.factorial(2 * i + 1)
    return sine * r, cosine


def per_row(scalars, shape, per_token):
    row = lax.broadcasted_iota(jnp.int32, shape, 0)
    column = jnp.full(shape, scalars[-1])
    for t in range(len(scalars) - 2, -1, -1):
        column = jnp.where(row < (t + 1) * per_token, scalars[t], column)
    return column


def turned(rope, positions):
    rows = rope.shape[0]
    half = ROPE // 2
    lane = lax.broadcasted_iota(jnp.int32, (1, ROPE), 1)
    frequency = jnp.zeros((1, ROPE), jnp.float32)
    for i in range(half):
        frequency = jnp.where(lane % half == i, THETA ** (-2.0 * i / ROPE), frequency)
    position = per_row(positions, (rows, ROPE), rows // DRAFT).astype(jnp.float32)
    sine, cosine = sine_cosine(position * frequency)
    swapped = jnp.concatenate([rope[:, half:], rope[:, :half]], axis=1)
    return rope * cosine + jnp.where(lane < half, -swapped, swapped) * sine


def kernel(
    sizes,
    lengths, offsets, q_hbm, keys_hbm, w_uv_hbm, w_out_hbm,
    out,
    q_raw, q_all, keys, values, w_uv, w_out, own, part_out, part_in, lse_out, lse_in,
    attended, heads_all, sums, sums_out, sums_in,
    load_sem, q_send, q_recv, part_send, part_recv, lse_send, lse_recv,
    heads_send, heads_recv, sums_send, sums_recv,
):
    n_ctx, n_seq, n_head = sizes
    ctx, seq, head = lax.axis_index("ctx"), lax.axis_index("seq"), lax.axis_index("head")
    rows, entries = q_raw.shape
    latent, places = own.shape[1], keys.shape[1]
    per_token = rows // DRAFT
    n_out = n_ctx * n_head
    place = ctx * n_head + head

    load_q = pltpu.make_async_copy(q_hbm, q_raw, load_sem.at[0])
    load_keys = pltpu.make_async_copy(keys_hbm, keys, load_sem.at[1])
    load_uv = pltpu.make_async_copy(w_uv_hbm, w_uv, load_sem.at[2])
    load_out = pltpu.make_async_copy(w_out_hbm, w_out, load_sem.at[3])
    load_q.start()
    load_keys.start()

    def row_device(k):
        other = lax.rem(place + k, n_out)
        return other, {"ctx": other // n_head, "head": lax.rem(other, n_head)}

    barrier = pltpu.get_barrier_semaphore()
    for k in range(1, n_out):
        pl.semaphore_signal(barrier, inc=1, device_id=row_device(k)[1], device_id_type=MESH)
    for k in range(1, n_seq):
        pl.semaphore_signal(
            barrier, inc=1, device_id={"seq": lax.rem(seq + k, n_seq)}, device_id_type=MESH
        )

    positions = [lengths[0] - DRAFT + offsets[0, t] for t in range(DRAFT)]
    limits = per_row(positions, (rows, 1), per_token)
    load_q.wait()
    latent_q = q_raw[:, :latent]
    rope_q = turned(q_raw[:, latent:].astype(jnp.float32), positions).astype(jnp.bfloat16)
    q_all[ctx, :, :latent] = latent_q
    q_all[ctx, :, latent:] = rope_q

    pl.semaphore_wait(barrier, n_out - 1 + n_seq - 1)

    toward = jnp.where(ctx < n_ctx // 2, 1, -1)
    shorter = jnp.minimum(ctx, n_ctx - 1 - ctx)

    def peer(k):
        near = jnp.where(lax.rem(k, 2) == 1, (k + 1) // 2, -(k // 2))
        return ctx + toward * jnp.where(k <= 2 * shorter, near, k - shorter)

    def q_copy(owner, side, send):
        return pltpu.make_async_remote_copy(
            src_ref=q_all.at[owner], dst_ref=q_all.at[owner],
            send_sem=q_send.at[send], recv_sem=q_recv.at[owner],
            device_id={"ctx": ctx + side}, device_id_type=MESH,
        )

    has_left, has_right = ctx > 0, ctx < n_ctx - 1

    @pl.when(has_right)
    def _():
        q_copy(ctx, 1, ctx).start()

    @pl.when(has_left)
    def _():
        q_copy(ctx, -1, n_ctx).start()

    def pass_on(distance):
        @pl.when(ctx - distance >= 0)
        def _():
            q_copy(ctx - distance, -1, 0).wait_recv()

            @pl.when(has_right)
            def _():
                q_copy(ctx - distance, 1, ctx - distance).start()

        @pl.when(ctx + distance < n_ctx)
        def _():
            q_copy(ctx + distance, 1, 0).wait_recv()

            @pl.when(has_left)
            def _():
                q_copy(ctx + distance, -1, ctx + distance).start()

    def part_copy(k, slot):
        return pltpu.make_async_remote_copy(
            src_ref=part_out.at[k], dst_ref=part_in.at[slot],
            send_sem=part_send.at[k], recv_sem=part_recv.at[slot],
            device_id={"ctx": peer(k)}, device_id_type=MESH,
        )

    def lse_copy(k, slot):
        return pltpu.make_async_remote_copy(
            src_ref=lse_out.at[k], dst_ref=lse_in.at[slot],
            send_sem=lse_send.at[k], recv_sem=lse_recv.at[slot],
            device_id={"ctx": peer(k)}, device_id_type=MESH,
        )

    load_keys.wait()
    load_uv.start()
    load_out.start()
    first_place = ctx * places

    def weigh(block):
        scores = jnp.dot(block, keys[...], preferred_element_type=jnp.float32)
        place_of = lax.broadcasted_iota(jnp.int32, (1, places), 1)
        scores = jnp.where(place_of <= limits - first_place, scores, NEGATIVE)
        maxima = jnp.max(scores, axis=1, keepdims=True)
        weights = jnp.exp2((scores - maxima) * (SCALE / LN2))
        totals = jnp.sum(weights, axis=1, keepdims=True)
        return weights.astype(jnp.bfloat16), 1.0 / totals, maxima * SCALE + jnp.log(totals)

    def attend_own(block):
        weights, inverse, lse = weigh(block)
        tile = next(c for c in (256, LANES) if places % c == 0)
        row = lax.broadcasted_iota(jnp.int32, (tile, tile), 0)
        column = lax.broadcasted_iota(jnp.int32, (tile, tile), 1)
        identity = (row == column).astype(jnp.float32).astype(jnp.bfloat16)
        numerators = jnp.zeros((rows, latent), jnp.float32)
        for begin in range(0, places, tile):
            some = slice(begin, begin + tile)
            product = lax.dot_general(
                jnp.concatenate([identity, weights[:, some]], axis=0), keys[:latent, some],
                (((1,), (1,)), ((), ())), preferred_element_type=jnp.float32,
            )
            values[some, :] = product[:tile].astype(jnp.bfloat16)
            numerators = numerators + product[tile:]
        return numerators * inverse, lse

    def attend(block):
        weights, inverse, lse = weigh(block)
        return jnp.dot(weights, values[...], preferred_element_type=jnp.float32) * inverse, lse

    diagonal = lax.broadcasted_iota(jnp.int32, (rows, rows), 0) == lax.broadcasted_iota(
        jnp.int32, (rows, rows), 1
    )

    def send_part(k, part, lse):
        part_out[k] = part.astype(jnp.bfloat16)
        as_row = jnp.sum(jnp.where(diagonal, lse, 0.0), axis=0, keepdims=True)
        lse_out[k] = jnp.broadcast_to(as_row, lse_out.shape[1:])
        part_copy(k, ctx).start()
        lse_copy(k, ctx).start()

    def remote_block(k, carried):
        pass_on(k)
        send_part(k, *attend(q_all[peer(k)]))
        return carried

    own_part, own_lse = attend_own(q_all[ctx])
    own[...] = own_part
    lax.fori_loop(1, n_ctx, remote_block, 0)

    top = own_lse
    lses = []
    for k in range(1, n_ctx):
        slot = peer(k)
        lse_copy(k, slot).wait_recv()
        lse = jnp.sum(
            jnp.where(diagonal, lse_in[slot, 0:1, :], 0.0), axis=1, keepdims=True
        )
        lses.append(lse)
        top = jnp.maximum(top, lse)
    share = jnp.exp(own_lse - top)
    whole = share
    mixed = own[...] * share
    for k in range(1, n_ctx):
        slot = peer(k)
        part_copy(k, slot).wait_recv()
        share = jnp.exp(lses[k - 1] - top)
        whole = whole + share
        mixed = mixed + part_in[slot].astype(jnp.float32) * share
    mixed = mixed / whole
    for t in range(DRAFT):
        attended[t] = mixed[t * per_token : (t + 1) * per_token]

    load_uv.wait()
    vdim = w_uv.shape[2]
    for h in range(per_token):
        heads_all[seq, :, h * vdim : (h + 1) * vdim] = jnp.dot(
            attended[:, h, :].astype(jnp.bfloat16), w_uv[h], preferred_element_type=jnp.float32
        )

    def heads_copy(k, slot):
        return pltpu.make_async_remote_copy(
            src_ref=heads_all.at[seq], dst_ref=heads_all.at[slot],
            send_sem=heads_send.at[k], recv_sem=heads_recv.at[slot],
            device_id={"seq": lax.rem(seq + k, n_seq)}, device_id_type=MESH,
        )

    for k in range(1, n_seq):
        heads_copy(k, seq).start()
    columns = w_out.shape[1]
    n_parts = sums.shape[0]
    part_columns = columns // n_parts
    part_blocks = part_columns // LANES
    sums[...] = jnp.zeros_like(sums)
    load_out.wait()
    for k in range(1, n_seq):
        heads_copy(k, lax.rem(seq + k, n_seq)).wait_recv()
    tokens = jnp.concatenate([heads_all[s] for s in range(n_seq)], axis=0).astype(jnp.bfloat16)
    width = next(c for c in (4 * LANES, 2 * LANES, LANES) if part_columns % c == 0)

    def sums_copy(part, k, target, slot):
        return pltpu.make_async_remote_copy(
            src_ref=sums_out.at[part, target], dst_ref=sums_in.at[part, slot],
            send_sem=sums_send.at[part, k], recv_sem=sums_recv.at[part, slot],
            device_id=row_device(k)[1], device_id_type=MESH,
        )

    for part in range(n_parts):
        for first in range(0, part_columns, width):
            begin = part * part_columns + first
            product = jnp.dot(
                tokens, w_out[:, begin : begin + width], preferred_element_type=jnp.float32
            )
            for r in range(n_out):
                for i in range(width // LANES):
                    sums[part, r, first // LANES + i, :] = product[r, i * LANES : (i + 1) * LANES]
        for k in range(1, n_out):
            target = row_device(k)[0]
            sums_out[part, target] = sums[part, target].astype(jnp.bfloat16)
            sums_copy(part, k, target, place).start()
    for part in range(n_parts):
        result = sums[part, place]
        for k in range(1, n_out):
            slot = row_device(k)[0]
            sums_copy(part, k, slot, slot).wait_recv()
            result = result + sums_in[part, slot].astype(jnp.float32)
        for i in range(part_blocks):
            begin = part * part_columns + i * LANES
            out[:, begin : begin + LANES] = result[i : i + 1].astype(jnp.bfloat16)

    @pl.when(has_right)
    def _():
        q_copy(ctx, 1, ctx).wait_send()

    @pl.when(has_left)
    def _():
        q_copy(ctx, -1, n_ctx).wait_send()

    for k in range(1, n_ctx):
        @pl.when((ctx - k >= 0) & has_right)
        def _():
            q_copy(ctx - k, 1, ctx - k).wait_send()

        @pl.when((ctx + k < n_ctx) & has_left)
        def _():
            q_copy(ctx + k, -1, ctx + k).wait_send()

        part_copy(k, ctx).wait_send()
        lse_copy(k, ctx).wait_send()
    for k in range(1, n_seq):
        heads_copy(k, seq).wait_send()
    for part in range(n_parts):
        for k in range(1, n_out):
            sums_copy(part, k, row_device(k)[0], place).wait_send()


def per_device(sizes, queries, cache, lengths, offsets, w_uv, w_out):
    n_ctx, n_seq, n_head = sizes
    n_out = n_ctx * n_head
    heads, entries = queries.shape[2:]
    rows = DRAFT * heads
    places = cache.shape[1]
    latent, vdim = w_uv.shape[1:]
    columns = w_out.shape[1]
    n_blocks = columns // LANES
    n_parts = 1
    padded = -(-n_blocks // n_parts // 16) * 16
    sixteen, full = jnp.bfloat16, jnp.float32
    dma = pltpu.SemaphoreType.DMA
    smem = pl.BlockSpec(memory_space=pltpu.SMEM)
    anywhere = pl.BlockSpec(memory_space=pl.ANY)
    return pl.pallas_call(
        functools.partial(kernel, sizes),
        out_shape=jax.ShapeDtypeStruct((1, columns), sixteen),
        in_specs=[smem, smem, anywhere, anywhere, anywhere, anywhere],
        out_specs=pl.BlockSpec(memory_space=pltpu.VMEM),
        scratch_shapes=[
            pltpu.VMEM((rows, entries), sixteen),
            pltpu.VMEM((n_ctx, rows, entries), sixteen),
            pltpu.VMEM((entries, places), sixteen),
            pltpu.VMEM((places, latent), sixteen),
            pltpu.VMEM(w_uv.shape, sixteen),
            pltpu.VMEM(w_out.shape, sixteen),
            pltpu.VMEM((rows, latent), full),
            pltpu.VMEM((n_ctx, rows, latent), sixteen),
            pltpu.VMEM((n_ctx, rows, latent), sixteen),
            pltpu.VMEM((n_ctx, 8, rows), full),
            pltpu.VMEM((n_ctx, 8, rows), full),
            pltpu.VMEM((DRAFT, heads, latent), full),
            pltpu.VMEM((n_seq, DRAFT, heads * vdim), full),
            pltpu.VMEM((n_parts, n_out, padded, LANES), full),
            pltpu.VMEM((n_parts, n_out, padded, LANES), sixteen),
            pltpu.VMEM((n_parts, n_out, padded, LANES), sixteen),
            dma((4,)),
            dma((n_ctx + 1,)), dma((n_ctx,)),
            dma((n_ctx,)), dma((n_ctx,)),
            dma((n_ctx,)), dma((n_ctx,)),
            dma((n_seq,)), dma((n_seq,)),
            dma((n_parts, n_out)), dma((n_parts, n_out)),
        ],
        compiler_params=pltpu.CompilerParams(
            collective_id=0, has_side_effects=True, vmem_limit_bytes=60 * 2**20
        ),
        name="latent_attention",
    )(
        lengths,
        offsets,
        queries.reshape(rows, entries),
        jnp.swapaxes(cache[0], 0, 1),
        w_uv,
        w_out,
    )


def solution(mesh):
    sizes = (mesh.shape["ctx"], mesh.shape["seq"], mesh.shape["head"])
    in_specs = (
        P(("groups", "seq"), None, ("ctx", "head"), None),
        P(("groups", "seq"), "ctx", None),
        P(("groups", "seq")),
        P(("groups", "seq"), None),
        P(("ctx", "head"), None, None),
        P(("ctx", "head"), "seq"),
    )
    out_specs = P(("groups", "ctx", "head"), "seq")
    return jax.shard_map(
        functools.partial(per_device, sizes),
        mesh=mesh, in_specs=in_specs, out_specs=out_specs, check_vma=False,
    )
```

```python
import functools
import math

import jax
import jax.numpy as jnp
from jax import lax
from jax.experimental import pallas as pl
from jax.experimental.pallas import tpu as pltpu
from jax.sharding import PartitionSpec as P

ROPE = 64
NOPE = 128
DRAFT = 4
LANES = 128
THETA = 10000.0
NEGATIVE = -1e30
SCALE = (NOPE + ROPE) ** -0.5
LN2 = math.log(2.0)
TURN = 2.0 * math.pi
TURN_HIGH = 6.28125
TURN_MID = math.floor((TURN - TURN_HIGH) * 2**19) / 2**19
TURN_LOW = TURN - TURN_HIGH - TURN_MID
MESH = pl.DeviceIdType.MESH


def sine_cosine(angle):
    turns = jnp.floor(angle * (1.0 / TURN) + 0.5)
    r = ((angle - turns * TURN_HIGH) - turns * TURN_MID) - turns * TURN_LOW
    square = r * r
    sine = jnp.zeros_like(r)
    cosine = jnp.zeros_like(r)
    for i in range(9, -1, -1):
        sign = -1.0 if i % 2 else 1.0
        cosine = cosine * square + sign / math.factorial(2 * i)
        sine = sine * square + sign / math.factorial(2 * i + 1)
    return sine * r, cosine


def per_row(scalars, shape, per_token):
    row = lax.broadcasted_iota(jnp.int32, shape, 0)
    column = jnp.full(shape, scalars[-1])
    for t in range(len(scalars) - 2, -1, -1):
        column = jnp.where(row < (t + 1) * per_token, scalars[t], column)
    return column


def turned(rope, positions):
    rows = rope.shape[0]
    half = ROPE // 2
    lane = lax.broadcasted_iota(jnp.int32, (1, ROPE), 1)
    frequency = jnp.zeros((1, ROPE), jnp.float32)
    for i in range(half):
        frequency = jnp.where(lane % half == i, THETA ** (-2.0 * i / ROPE), frequency)
    position = per_row(positions, (rows, ROPE), rows // DRAFT).astype(jnp.float32)
    sine, cosine = sine_cosine(position * frequency)
    swapped = jnp.concatenate([rope[:, half:], rope[:, :half]], axis=1)
    return rope * cosine + jnp.where(lane < half, -swapped, swapped) * sine


def kernel(
    sizes,
    lengths, offsets, q_hbm, keys_hbm, w_uv_hbm, w_out_hbm,
    out,
    q_raw, q_all, keys, values, w_uv, w_out, own, part_out, part_in, lse_out, lse_in,
    attended, heads_all, sums, sums_out, sums_in,
    load_sem, q_send, q_recv, part_send, part_recv, lse_send, lse_recv,
    heads_send, heads_recv, sums_send, sums_recv,
):
    n_ctx, n_seq, n_head = sizes
    ctx, seq, head = lax.axis_index("ctx"), lax.axis_index("seq"), lax.axis_index("head")
    rows, entries = q_raw.shape
    latent, places = own.shape[1], keys.shape[1]
    per_token = rows // DRAFT
    n_out = n_ctx * n_head
    place = ctx * n_head + head

    load_q = pltpu.make_async_copy(q_hbm, q_raw, load_sem.at[0])
    band = entries // 4
    load_keys = [
        pltpu.make_async_copy(
            keys_hbm.at[pl.ds(i * band, band)], keys.at[pl.ds(i * band, band)], load_sem.at[4 + i]
        )
        for i in range(4)
    ]
    load_uv = pltpu.make_async_copy(w_uv_hbm, w_uv, load_sem.at[2])
    load_out = pltpu.make_async_copy(w_out_hbm, w_out, load_sem.at[3])
    load_q.start()
    for copy in load_keys:
        copy.start()

    def row_device(k):
        other = lax.rem(place + k, n_out)
        return other, {"ctx": other // n_head, "head": lax.rem(other, n_head)}

    barrier = pltpu.get_barrier_semaphore()
    for k in range(1, n_out):
        pl.semaphore_signal(barrier, inc=1, device_id=row_device(k)[1], device_id_type=MESH)
    for k in range(1, n_seq):
        pl.semaphore_signal(
            barrier, inc=1, device_id={"seq": lax.rem(seq + k, n_seq)}, device_id_type=MESH
        )

    positions = [lengths[0] - DRAFT + offsets[0, t] for t in range(DRAFT)]
    limits = per_row(positions, (rows, 1), per_token)
    load_q.wait()
    latent_q = q_raw[:, :latent]
    rope_q = turned(q_raw[:, latent:].astype(jnp.float32), positions).astype(jnp.bfloat16)
    q_all[ctx, :, :latent] = latent_q
    q_all[ctx, :, latent:] = rope_q

    pl.semaphore_wait(barrier, n_out - 1 + n_seq - 1)

    toward = jnp.where(ctx < n_ctx // 2, 1, -1)
    shorter = jnp.minimum(ctx, n_ctx - 1 - ctx)

    def peer(k):
        near = jnp.where(lax.rem(k, 2) == 1, (k + 1) // 2, -(k // 2))
        return ctx + toward * jnp.where(k <= 2 * shorter, near, k - shorter)

    def q_copy(owner, side, send):
        return pltpu.make_async_remote_copy(
            src_ref=q_all.at[owner], dst_ref=q_all.at[owner],
            send_sem=q_send.at[send], recv_sem=q_recv.at[owner],
            device_id={"ctx": ctx + side}, device_id_type=MESH,
        )

    has_left, has_right = ctx > 0, ctx < n_ctx - 1

    @pl.when(has_right)
    def _():
        q_copy(ctx, 1, ctx).start()

    @pl.when(has_left)
    def _():
        q_copy(ctx, -1, n_ctx).start()

    def pass_on(distance):
        @pl.when(ctx - distance >= 0)
        def _():
            q_copy(ctx - distance, -1, 0).wait_recv()

            @pl.when(has_right)
            def _():
                q_copy(ctx - distance, 1, ctx - distance).start()

        @pl.when(ctx + distance < n_ctx)
        def _():
            q_copy(ctx + distance, 1, 0).wait_recv()

            @pl.when(has_left)
            def _():
                q_copy(ctx + distance, -1, ctx + distance).start()

    def part_copy(k, slot):
        return pltpu.make_async_remote_copy(
            src_ref=part_out.at[k], dst_ref=part_in.at[slot],
            send_sem=part_send.at[k], recv_sem=part_recv.at[slot],
            device_id={"ctx": peer(k)}, device_id_type=MESH,
        )

    def lse_copy(k, slot):
        return pltpu.make_async_remote_copy(
            src_ref=lse_out.at[k], dst_ref=lse_in.at[slot],
            send_sem=lse_send.at[k], recv_sem=lse_recv.at[slot],
            device_id={"ctx": peer(k)}, device_id_type=MESH,
        )

    for copy in load_keys:
        copy.wait()
    load_uv.start()
    load_out.start()
    first_place = ctx * places

    def weigh(block):
        scores = jnp.dot(block, keys[...], preferred_element_type=jnp.float32)
        place_of = lax.broadcasted_iota(jnp.int32, (1, places), 1)
        scores = jnp.where(place_of <= limits - first_place, scores, NEGATIVE)
        maxima = jnp.max(scores, axis=1, keepdims=True)
        weights = jnp.exp2((scores - maxima) * (SCALE / LN2))
        totals = jnp.sum(weights, axis=1, keepdims=True)
        return weights.astype(jnp.bfloat16), 1.0 / totals, maxima * SCALE + jnp.log(totals)

    def attend_own(block):
        weights, inverse, lse = weigh(block)
        tile = next(c for c in (256, LANES) if places % c == 0)
        row = lax.broadcasted_iota(jnp.int32, (tile, tile), 0)
        column = lax.broadcasted_iota(jnp.int32, (tile, tile), 1)
        identity = (row == column).astype(jnp.float32).astype(jnp.bfloat16)
        numerators = jnp.zeros((rows, latent), jnp.float32)
        for begin in range(0, places, tile):
            some = slice(begin, begin + tile)
            product = lax.dot_general(
                jnp.concatenate([identity, weights[:, some]], axis=0), keys[:latent, some],
                (((1,), (1,)), ((), ())), preferred_element_type=jnp.float32,
            )
            values[some, :] = product[:tile].astype(jnp.bfloat16)
            numerators = numerators + product[tile:]
        return numerators * inverse, lse

    def attend(block):
        weights, inverse, lse = weigh(block)
        return jnp.dot(weights, values[...], preferred_element_type=jnp.float32) * inverse, lse

    diagonal = lax.broadcasted_iota(jnp.int32, (rows, rows), 0) == lax.broadcasted_iota(
        jnp.int32, (rows, rows), 1
    )

    def send_part(k, part, lse):
        part_out[k] = part.astype(jnp.bfloat16)
        as_row = jnp.sum(jnp.where(diagonal, lse, 0.0), axis=0, keepdims=True)
        lse_out[k] = jnp.broadcast_to(as_row, lse_out.shape[1:])
        part_copy(k, ctx).start()
        lse_copy(k, ctx).start()

    def remote_block(k, carried):
        pass_on(k)
        send_part(k, *attend(q_all[peer(k)]))
        return carried

    own_part, own_lse = attend_own(q_all[ctx])
    own[...] = own_part
    lax.fori_loop(1, n_ctx, remote_block, 0)

    top = own_lse
    lses = []
    for k in range(1, n_ctx):
        slot = peer(k)
        lse_copy(k, slot).wait_recv()
        lse = jnp.sum(
            jnp.where(diagonal, lse_in[slot, 0:1, :], 0.0), axis=1, keepdims=True
        )
        lses.append(lse)
        top = jnp.maximum(top, lse)
    share = jnp.exp(own_lse - top)
    whole = share
    mixed = own[...] * share
    for k in range(1, n_ctx):
        slot = peer(k)
        part_copy(k, slot).wait_recv()
        share = jnp.exp(lses[k - 1] - top)
        whole = whole + share
        mixed = mixed + part_in[slot].astype(jnp.float32) * share
    mixed = mixed / whole
    for t in range(DRAFT):
        attended[t] = mixed[t * per_token : (t + 1) * per_token]

    load_uv.wait()
    vdim = w_uv.shape[2]
    for h in range(per_token):
        heads_all[seq, :, h * vdim : (h + 1) * vdim] = jnp.dot(
            attended[:, h, :].astype(jnp.bfloat16), w_uv[h], preferred_element_type=jnp.float32
        )

    def heads_copy(k, slot):
        return pltpu.make_async_remote_copy(
            src_ref=heads_all.at[seq], dst_ref=heads_all.at[slot],
            send_sem=heads_send.at[k], recv_sem=heads_recv.at[slot],
            device_id={"seq": lax.rem(seq + k, n_seq)}, device_id_type=MESH,
        )

    for k in range(1, n_seq):
        heads_copy(k, seq).start()
    columns = w_out.shape[1]
    n_parts = sums.shape[0]
    part_columns = columns // n_parts
    part_blocks = part_columns // LANES
    sums[...] = jnp.zeros_like(sums)
    load_out.wait()
    for k in range(1, n_seq):
        heads_copy(k, lax.rem(seq + k, n_seq)).wait_recv()
    tokens = jnp.concatenate([heads_all[s] for s in range(n_seq)], axis=0).astype(jnp.bfloat16)
    width = next(c for c in (4 * LANES, 2 * LANES, LANES) if part_columns % c == 0)

    def sums_copy(part, k, target, slot):
        return pltpu.make_async_remote_copy(
            src_ref=sums_out.at[part, target], dst_ref=sums_in.at[part, slot],
            send_sem=sums_send.at[part, k], recv_sem=sums_recv.at[part, slot],
            device_id=row_device(k)[1], device_id_type=MESH,
        )

    for part in range(n_parts):
        for first in range(0, part_columns, width):
            begin = part * part_columns + first
            product = jnp.dot(
                tokens, w_out[:, begin : begin + width], preferred_element_type=jnp.float32
            )
            for r in range(n_out):
                for i in range(width // LANES):
                    sums[part, r, first // LANES + i, :] = product[r, i * LANES : (i + 1) * LANES]
        for k in range(1, n_out):
            target = row_device(k)[0]
            sums_out[part, target] = sums[part, target].astype(jnp.bfloat16)
            sums_copy(part, k, target, place).start()
    for part in range(n_parts):
        result = sums[part, place]
        for k in range(1, n_out):
            slot = row_device(k)[0]
            sums_copy(part, k, slot, slot).wait_recv()
            result = result + sums_in[part, slot].astype(jnp.float32)
        for i in range(part_blocks):
            begin = part * part_columns + i * LANES
            out[:, begin : begin + LANES] = result[i : i + 1].astype(jnp.bfloat16)

    @pl.when(has_right)
    def _():
        q_copy(ctx, 1, ctx).wait_send()

    @pl.when(has_left)
    def _():
        q_copy(ctx, -1, n_ctx).wait_send()

    for k in range(1, n_ctx):
        @pl.when((ctx - k >= 0) & has_right)
        def _():
            q_copy(ctx - k, 1, ctx - k).wait_send()

        @pl.when((ctx + k < n_ctx) & has_left)
        def _():
            q_copy(ctx + k, -1, ctx + k).wait_send()

        part_copy(k, ctx).wait_send()
        lse_copy(k, ctx).wait_send()
    for k in range(1, n_seq):
        heads_copy(k, seq).wait_send()
    for part in range(n_parts):
        for k in range(1, n_out):
            sums_copy(part, k, row_device(k)[0], place).wait_send()


def per_device(sizes, queries, cache, lengths, offsets, w_uv, w_out):
    n_ctx, n_seq, n_head = sizes
    n_out = n_ctx * n_head
    heads, entries = queries.shape[2:]
    rows = DRAFT * heads
    places = cache.shape[1]
    latent, vdim = w_uv.shape[1:]
    columns = w_out.shape[1]
    n_blocks = columns // LANES
    n_parts = 1
    padded = -(-n_blocks // n_parts // 16) * 16
    sixteen, full = jnp.bfloat16, jnp.float32
    dma = pltpu.SemaphoreType.DMA
    smem = pl.BlockSpec(memory_space=pltpu.SMEM)
    anywhere = pl.BlockSpec(memory_space=pl.ANY)
    return pl.pallas_call(
        functools.partial(kernel, sizes),
        out_shape=jax.ShapeDtypeStruct((1, columns), sixteen),
        in_specs=[smem, smem, anywhere, anywhere, anywhere, anywhere],
        out_specs=pl.BlockSpec(memory_space=pltpu.VMEM),
        scratch_shapes=[
            pltpu.VMEM((rows, entries), sixteen),
            pltpu.VMEM((n_ctx, rows, entries), sixteen),
            pltpu.VMEM((entries, places), sixteen),
            pltpu.VMEM((places, latent), sixteen),
            pltpu.VMEM(w_uv.shape, sixteen),
            pltpu.VMEM(w_out.shape, sixteen),
            pltpu.VMEM((rows, latent), full),
            pltpu.VMEM((n_ctx, rows, latent), sixteen),
            pltpu.VMEM((n_ctx, rows, latent), sixteen),
            pltpu.VMEM((n_ctx, 8, rows), full),
            pltpu.VMEM((n_ctx, 8, rows), full),
            pltpu.VMEM((DRAFT, heads, latent), full),
            pltpu.VMEM((n_seq, DRAFT, heads * vdim), full),
            pltpu.VMEM((n_parts, n_out, padded, LANES), full),
            pltpu.VMEM((n_parts, n_out, padded, LANES), sixteen),
            pltpu.VMEM((n_parts, n_out, padded, LANES), sixteen),
            dma((8,)),
            dma((n_ctx + 1,)), dma((n_ctx,)),
            dma((n_ctx,)), dma((n_ctx,)),
            dma((n_ctx,)), dma((n_ctx,)),
            dma((n_seq,)), dma((n_seq,)),
            dma((n_parts, n_out)), dma((n_parts, n_out)),
        ],
        compiler_params=pltpu.CompilerParams(
            collective_id=0, has_side_effects=True, vmem_limit_bytes=60 * 2**20
        ),
        name="latent_attention",
    )(
        lengths,
        offsets,
        queries.reshape(rows, entries),
        jnp.swapaxes(cache[0], 0, 1),
        w_uv,
        w_out,
    )


def solution(mesh):
    sizes = (mesh.shape["ctx"], mesh.shape["seq"], mesh.shape["head"])
    in_specs = (
        P(("groups", "seq"), None, ("ctx", "head"), None),
        P(("groups", "seq"), "ctx", None),
        P(("groups", "seq")),
        P(("groups", "seq"), None),
        P(("ctx", "head"), None, None),
        P(("ctx", "head"), "seq"),
    )
    out_specs = P(("groups", "ctx", "head"), "seq")
    return jax.shard_map(
        functools.partial(per_device, sizes),
        mesh=mesh, in_specs=in_specs, out_specs=out_specs, check_vma=False,
    )
```
